512 devices in a mesh: seq: 16 (over x, y_lo, core), mp: 32 (over y_hi, z).
Axes of the slice: x: 4, y: 4 (y_hi: 2, y_lo: 2; y = y_hi * 2 + y_lo), z: 16, core: 2. Of those that a mesh axis runs over, the one named last changes fastest.
Arguments:
- tokens: bfloat16 [2048, 8192], P('seq', 'mp'), may hold values from -6 to 6
- block_values: bfloat16 [256, 16, 128, 128], P('mp', 'seq'), may hold values from -0.125 to 0.125
- block_rows: int32 [256, 16], P('mp', 'seq'), may hold values from 0 to 63, as said below
- grad_act: bfloat16 [2048, 32768], P('seq', 'mp'), may hold values from -1.5 to 1.5
Outputs:
- activated: bfloat16 [2048, 32768], P('seq', 'mp')
- grad_tokens: bfloat16 [2048, 8192], P('seq', 'mp')
- grad_values: bfloat16 [256, 16, 128, 128], P('mp', 'seq')
The draws below stay inside these ranges and needn't reach their ends.
Inputs may be any that keep to these rules, and one draw needn't show every extreme that they name: `block_rows`: each block column names 16 different block rows.
All inputs are finite; a program needn't handle non-finite values.
Results may differ from the reference program's by a relative error of at most 0.023.
Values may be sent and summed in bfloat16 or wider, within the bound.
No kernel may reach another device: no remote copies, remote signals or barrier semaphores. Data moves between devices by JAX's collectives and lax.ppermute only.
A program may use at most 64 MiB of HBM per device.

```python
import jax
import jax.numpy as jnp
from jax import lax

D = 8192
FF = 32768
BLOCK = 128
KEPT = 16
TOKENS = 2048
BLOCK_COLS = 256
COLS_DEV = 8
N_MP = 32


def draw_block_rows(key, part):
    key = jax.random.fold_in(key, 11)
    row_count = D // BLOCK
    scores = jax.random.randint(key, (BLOCK_COLS, row_count), 0, 1 << 20)
    scores = scores * row_count + jnp.arange(row_count, dtype=jnp.int32)[None, :]
    return lax.top_k(scores, KEPT)[1].astype(jnp.int32)


def block_scale(own_key, extent, cuts, least, largest):
    factor_of, own = 1.0, jax.random.fold_in(own_key, 6)
    for dim, parts in cuts:
        steps = jnp.exp(jax.random.uniform(jax.random.fold_in(own, dim), (parts,), jnp.float32, least / len(cuts), largest / len(cuts)))
        factor_of = factor_of * jnp.repeat(steps, extent[dim] // parts).reshape([-1 if axis == dim else 1 for axis in range(len(extent))])
    return factor_of


def bell_draw(rng, shape, spread, bound, pieces=(), held_as=jnp.bfloat16):
    values = spread * jax.random.normal(rng, shape, jnp.float32)
    if pieces:
        values = values * block_scale(rng, shape, pieces, -0.22, 0.18)
    return jnp.clip(values, -bound, bound).astype(held_as)


def setup_inputs(seed: int = 0) -> dict:
    arg_keys = jax.random.split(jax.random.key(seed), 5)
    return {
        "tokens": bell_draw(arg_keys[0], (TOKENS, D), 1.0, 6.0, ((0, 16), (1, 32))),
        "block_values": bell_draw(arg_keys[1], (BLOCK_COLS, KEPT, BLOCK, BLOCK), (KEPT * BLOCK) ** -0.5, 0.125, ((0, 32), (1, 16))),
        "block_rows": draw_block_rows(jax.random.fold_in(arg_keys[4], 71), 0),
        "grad_act": bell_draw(arg_keys[3], (TOKENS, FF), 0.25, 1.5, ((0, 16), (1, 32))),
    }


SQRT_TWO_PI = 0.7978845608028654
CUBIC = 0.044715


def gelu_parts(hidden):
    inner_arg = SQRT_TWO_PI * (hidden + CUBIC * hidden * hidden * hidden)
    tanh_inner = jnp.tanh(inner_arg)
    gelu_value = 0.5 * hidden * (1.0 + tanh_inner)
    gelu_slope = 0.5 * (1.0 + tanh_inner) + 0.5 * hidden * (1.0 - tanh_inner * tanh_inner) * SQRT_TWO_PI * (1.0 + 3.0 * CUBIC * hidden * hidden)
    return gelu_value, gelu_slope


def reference(tokens, block_values, block_rows, grad_act):
    row_count = D // BLOCK
    row_blocks = tokens.reshape(TOKENS, row_count, BLOCK)
    values_grouped = block_values.reshape(N_MP, COLS_DEV, KEPT, BLOCK, BLOCK)
    rows_grouped = block_rows.reshape(N_MP, COLS_DEV, KEPT)
    grads_grouped = jnp.transpose(grad_act.reshape(TOKENS, N_MP, COLS_DEV, BLOCK), (1, 0, 2, 3))

    def group_step(running_sum, inputs):
        weights, row_ids, grad_piece = inputs
        picked = jnp.take(row_blocks, row_ids, axis=1).astype(jnp.float32)
        weight_f32 = weights.astype(jnp.float32)
        hidden = jnp.einsum("tckp,ckpq->tcq", picked, weight_f32)
        gelu_value, gelu_slope = gelu_parts(hidden)
        grad_hidden = (grad_piece.astype(jnp.float32) * gelu_slope).astype(jnp.bfloat16)
        grad_f32 = grad_hidden.astype(jnp.float32)
        slot_parts = jnp.einsum("tcq,ckpq->tckp", grad_f32, weight_f32)
        group_term = jnp.zeros((TOKENS, row_count, BLOCK), jnp.float32)
        group_term = group_term.at[:, row_ids.reshape(-1)].add(slot_parts.reshape(TOKENS, COLS_DEV * KEPT, BLOCK))
        rounded = lax.optimization_barrier(group_term.astype(jnp.bfloat16))
        running_sum = running_sum + rounded.astype(jnp.float32)
        slot_grads = jnp.einsum("tckp,tcq->ckpq", picked, grad_f32).astype(jnp.bfloat16)
        return running_sum, (gelu_value.astype(jnp.bfloat16), slot_grads)

    start_sum = jnp.zeros((TOKENS, row_count, BLOCK), jnp.float32)
    running_sum, (activated, slot_grads) = lax.scan(group_step, start_sum, (values_grouped, rows_grouped, grads_grouped))
    activated = jnp.transpose(activated, (1, 0, 2, 3)).reshape(TOKENS, FF)
    grad_tokens = running_sum.reshape(TOKENS, D).astype(jnp.bfloat16)
    grad_values = slot_grads.reshape(BLOCK_COLS, KEPT, BLOCK, BLOCK)
    return (activated, grad_tokens, grad_values)
```

```python
import jax
import jax.numpy as jnp
from jax import lax
from jax.experimental import pallas as pl
from jax.experimental.pallas import tpu as pltpu
from jax.sharding import Mesh
from jax.sharding import PartitionSpec as P

SQRT_TWO_PI = 0.7978845608028654
CUBIC = 0.044715
AXES = ("x", "yl", "core", "yh", "z")
SIZES = (4, 2, 2, 2, 16)
SEQ = ("x", "yl", "core")
MP = ("yh", "z")


def gelu_parts(hidden):
    inner_arg = SQRT_TWO_PI * (hidden + CUBIC * hidden * hidden * hidden)
    tanh_inner = jnp.tanh(inner_arg)
    gelu_value = 0.5 * hidden * (1.0 + tanh_inner)
    gelu_slope = 0.5 * (1.0 + tanh_inner) + 0.5 * hidden * (
        1.0 - tanh_inner * tanh_inner
    ) * SQRT_TWO_PI * (1.0 + 3.0 * CUBIC * hidden * hidden)
    return gelu_value, gelu_slope


def column_kernel(rows_ref, tok_ref, w_ref, gact_ref, act_ref, term_ref, gv_ref, acc, tok_t):
    c = pl.program_id(0)
    kept = w_ref.shape[0]

    @pl.when(c == 0)
    def _():
        acc[...] = jnp.zeros_like(acc)

        @pl.loop(0, tok_ref.shape[0])
        def _(r):
            tok_t[r] = tok_ref[r].T

    rows = [rows_ref[k, c] for k in range(kept)]
    weights = w_ref[...].reshape(kept * 128, 128)
    picked = jnp.concatenate([tok_ref[r] for r in rows], axis=1)
    hidden = jnp.dot(picked, weights, preferred_element_type=jnp.float32)
    value, slope = gelu_parts(hidden)
    act_ref[...] = value.astype(jnp.bfloat16)
    grad_hidden = (gact_ref[...].astype(jnp.float32) * slope).astype(jnp.bfloat16)
    for k in range(kept):
        acc[rows[k]] += lax.dot_general(
            grad_hidden, w_ref[k, 0], (((1,), (1,)), ((), ())), preferred_element_type=jnp.float32
        )
        gv_ref[k, 0] = jnp.dot(
            tok_t[rows[k]], grad_hidden, preferred_element_type=jnp.float32
        ).astype(jnp.bfloat16)

    @pl.when(c == pl.num_programs(0) - 1)
    def _():
        term_ref[...] = acc[...].astype(jnp.bfloat16)


def columns(rows, tok, weights, grad_act):
    n_rows, n_tok, block = tok.shape
    kept, cols = weights.shape[:2]
    return pl.pallas_call(
        column_kernel,
        grid_spec=pltpu.PrefetchScalarGridSpec(
            num_scalar_prefetch=1,
            grid=(cols,),
            in_specs=[
                pl.BlockSpec((n_rows, n_tok, block), lambda c, rows: (0, 0, 0)),
                pl.BlockSpec((kept, 1, block, block), lambda c, rows: (0, c, 0, 0)),
                pl.BlockSpec((n_tok, block), lambda c, rows: (0, c)),
            ],
            out_specs=[
                pl.BlockSpec((n_tok, block), lambda c, rows: (0, c)),
                pl.BlockSpec((n_rows, n_tok, block), lambda c, rows: (0, 0, 0)),
                pl.BlockSpec((kept, 1, block, block), lambda c, rows: (0, c, 0, 0)),
            ],
            scratch_shapes=[
                pltpu.VMEM((n_rows, n_tok, block), jnp.float32),
                pltpu.VMEM((n_rows, block, n_tok), jnp.bfloat16),
            ],
        ),
        out_shape=[
            jax.ShapeDtypeStruct((n_tok, cols * block), jnp.bfloat16),
            jax.ShapeDtypeStruct((n_rows, n_tok, block), jnp.bfloat16),
            jax.ShapeDtypeStruct((kept, cols, block, block), jnp.bfloat16),
        ],
        compiler_params=pltpu.CompilerParams(vmem_limit_bytes=40 * 2**20),
        cost_estimate=pl.CostEstimate(flops=1_610_612_736, bytes_accessed=13_000_000, transcendentals=131072),
    )(rows, tok, weights, grad_act)


def shards(tokens, block_values, block_rows, grad_act):
    n_tok = tokens.shape[0]
    cols, _, block, _ = block_values.shape
    mine = tokens.reshape(n_tok, 2, block).transpose(1, 0, 2)
    pair = lax.all_gather(mine, "yh", axis=0)
    tok = lax.all_gather(pair, "z", axis=0).reshape(64, n_tok, block)
    rows = lax.all_gather(block_rows.reshape(cols), SEQ, axis=0)
    weights = lax.all_gather(block_values.reshape(cols, block, block), SEQ, axis=0)
    rows = (rows % 32) // 2 * 4 + rows // 32 * 2 + rows % 2
    activated, term, gv = columns(rows, tok, weights, grad_act)
    gv = lax.all_to_all(gv, SEQ, 0, 0)
    gv = gv.astype(jnp.float32).sum(0).astype(jnp.bfloat16)
    part = lax.psum_scatter(term.reshape(16, 2, 2, n_tok, block), "z", scatter_dimension=0)
    yh = lax.axis_index("yh")
    keep = lax.dynamic_index_in_dim(part, yh, 0, keepdims=False)
    give = lax.dynamic_index_in_dim(part, 1 - yh, 0, keepdims=False)
    got = lax.ppermute(give, "yh", [(0, 1), (1, 0)])
    summed = (keep.astype(jnp.float32) + got.astype(jnp.float32)).astype(jnp.bfloat16)
    summed = summed.transpose(1, 0, 2).reshape(n_tok, 2 * block)
    return activated, summed, gv.reshape(cols, 1, block, block)


def solution(mesh):
    fine = Mesh(mesh.devices.reshape(SIZES), AXES)
    in_specs = (P(SEQ, MP), P(MP, SEQ, None, None), P(MP, SEQ), P(SEQ, MP))
    out_specs = (P(SEQ, MP), P(SEQ, MP), P(MP, SEQ, None, None))
    return jax.shard_map(shards, mesh=fine, in_specs=in_specs, out_specs=out_specs, check_vma=False)
```

```python
import jax
import jax.numpy as jnp
from jax import lax
from jax.experimental import pallas as pl
from jax.experimental.pallas import tpu as pltpu
from jax.sharding import Mesh
from jax.sharding import PartitionSpec as P

SQRT_TWO_PI = 0.7978845608028654
CUBIC = 0.044715
AXES = ("x", "yl", "core", "yh", "z")
SIZES = (4, 2, 2, 2, 16)
SEQ = ("x", "yl", "core")
MP = ("yh", "z")
BF16, F32 = jnp.bfloat16, jnp.float32
OWN, LEFT, RIGHT = (0, 4, 8, 12), (1, 5, 9, 13), (15, 3, 7, 11)
FAR_LEFT, FAR_RIGHT = (6, 10), (14, 2)
PARTS = (OWN, LEFT, RIGHT, FAR_LEFT, FAR_RIGHT)


def gelu_parts(hidden):
    inner_arg = SQRT_TWO_PI * (hidden + CUBIC * hidden * hidden * hidden)
    tanh_inner = jnp.tanh(inner_arg)
    gelu_value = 0.5 * hidden * (1.0 + tanh_inner)
    gelu_slope = 0.5 * (1.0 + tanh_inner) + 0.5 * hidden * (
        1.0 - tanh_inner * tanh_inner
    ) * SQRT_TWO_PI * (1.0 + 3.0 * CUBIC * hidden * hidden)
    return gelu_value, gelu_slope


def hidden_kernel(
    rows_ref, own, left, right, far_left, far_right, w_ref, gact_ref, act_ref, gh_ref, gv_ref, tok, sem
):
    c = pl.program_id(0)
    kept = gv_ref.shape[0]

    @pl.when(c == 0)
    def _():
        copies = [
            pltpu.make_async_copy(ref.at[i], tok.at[pl.ds(4 * d, 4)], sem.at[d])
            for ref, part in zip((own, left, right, far_left, far_right), PARTS)
            for i, d in enumerate(part)
        ]
        for copy in copies:
            copy.start()
        for copy in copies:
            copy.wait()

    rows = [rows_ref[k, c] for k in range(kept)]
    weights = w_ref[...].reshape(kept * 128, 128)
    picked = jnp.concatenate([tok[r] for r in rows], axis=1)
    hidden = jnp.dot(picked, weights, preferred_element_type=F32)
    value, slope = gelu_parts(hidden)
    act_ref[...] = value.astype(BF16)
    grad_hidden = (gact_ref[...].astype(F32) * slope).astype(BF16)
    gh_ref[...] = grad_hidden
    grads = lax.dot_general(
        grad_hidden, picked, (((0,), (0,)), ((), ())), preferred_element_type=F32
    ).astype(BF16)
    for k in range(kept):
        gv_ref[k, 0] = grads[:, k * 128 : (k + 1) * 128]


def term_kernel(rows_ref, gh_ref, w_ref, own, left, right, far_left, far_right, acc):
    c = pl.program_id(0)
    kept = w_ref.shape[0]

    @pl.when(c == 0)
    def _():
        acc[...] = jnp.zeros_like(acc)

    weights = w_ref[...].reshape(kept * 128, 128)
    part = lax.dot_general(
        gh_ref[...], weights, (((1,), (1,)), ((), ())), preferred_element_type=F32
    )
    for k in range(kept):
        acc[rows_ref[k, c]] += part[:, k * 128 : (k + 1) * 128]

    @pl.when(c == pl.num_programs(0) - 1)
    def _():
        for ref, places in zip((own, left, right, far_left, far_right), PARTS):
            for i, d in enumerate(places):
                ref[i] = acc[4 * d : 4 * d + 4].astype(BF16)


def hidden_call(rows, parts, weights, grad_act):
    kept, cols = rows.shape
    n_tok = grad_act.shape[0]
    column = pl.BlockSpec((n_tok, 128), lambda c, rows: (0, c))
    return pl.pallas_call(
        hidden_kernel,
        grid_spec=pltpu.PrefetchScalarGridSpec(
            num_scalar_prefetch=1,
            grid=(cols,),
            in_specs=[pl.BlockSpec(memory_space=pl.ANY)] * 5
            + [pl.BlockSpec((kept, 128, 128), lambda c, rows: (0, c, 0)), column],
            out_specs=[
                column,
                column,
                pl.BlockSpec((kept, 1, 128, 128), lambda c, rows: (0, c, 0, 0)),
            ],
            scratch_shapes=[pltpu.VMEM((64, n_tok, 128), BF16), pltpu.SemaphoreType.DMA((16,))],
        ),
        out_shape=[
            jax.ShapeDtypeStruct((n_tok, cols * 128), BF16),
            jax.ShapeDtypeStruct((n_tok, cols * 128), BF16),
            jax.ShapeDtypeStruct((kept, cols, 128, 128), BF16),
        ],
        compiler_params=pltpu.CompilerParams(vmem_limit_bytes=40 * 2**20),
        cost_estimate=pl.CostEstimate(flops=1_073_741_824, bytes_accessed=11_000_000, transcendentals=131072),
    )(rows, *parts, weights, grad_act)


def term_call(rows, grad_hidden, weights):
    kept, cols = rows.shape
    n_tok = grad_hidden.shape[0]
    return pl.pallas_call(
        term_kernel,
        grid_spec=pltpu.PrefetchScalarGridSpec(
            num_scalar_prefetch=1,
            grid=(cols,),
            in_specs=[
                pl.BlockSpec((n_tok, 128), lambda c, rows: (0, c)),
                pl.BlockSpec((kept, 128, 128), lambda c, rows: (0, c, 0)),
            ],
            out_specs=[
                pl.BlockSpec((len(p), 4, n_tok, 128), lambda c, rows: (0, 0, 0, 0)) for p in PARTS
            ],
            scratch_shapes=[pltpu.VMEM((64, n_tok, 128), F32)],
        ),
        out_shape=[jax.ShapeDtypeStruct((len(p), 4, n_tok, 128), BF16) for p in PARTS],
        compiler_params=pltpu.CompilerParams(vmem_limit_bytes=40 * 2**20),
        cost_estimate=pl.CostEstimate(flops=536_870_912, bytes_accessed=7_000_000, transcendentals=0),
    )(rows, grad_hidden, weights)


def shift(a, by):
    return lax.ppermute(a, "z", [(i, (i + by) % 16) for i in range(16)])


def swap(a, axis):
    return lax.ppermute(a, axis, [(0, 1), (1, 0)])


def total(*arrays):
    return sum(a.astype(F32) for a in arrays)


def gather_tokens(mine):
    quad = jnp.stack([mine, shift(mine, 4), shift(mine, 8), shift(mine, -4)])
    own = jnp.concatenate([quad, swap(quad, "yh")], axis=1)
    left, right = shift(own, 1), shift(own, -1)
    return own, left, right, shift(left[1:3], 1), shift(right[0:2], -1)


def reduce_terms(own, left, right, far_left, far_right):
    from_right, from_left = shift(far_left, -1), shift(far_right, 1)
    left = jnp.concatenate([left[:1], total(left[1:3], from_right).astype(BF16), left[3:]])
    right = jnp.concatenate([total(right[:2], from_left).astype(BF16), right[2:]])
    own = total(own, shift(left, -1), shift(right, 1)).astype(BF16)
    own = total(own[:, :2], swap(own[:, 2:], "yh")).astype(BF16)
    return total(own[0], shift(own[1], -4), shift(own[2], 8), shift(own[3], 4)).astype(BF16)


def shards(tokens, block_values, block_rows, grad_act):
    n_tok = tokens.shape[0]
    cols = block_values.shape[0]
    row_tile = jnp.zeros((16, 128), BF16).at[0, :cols].set(block_rows[:, 0].astype(BF16))
    sent = jnp.concatenate([block_values.reshape(cols * 128, 128), row_tile])
    weights = lax.all_gather(sent, SEQ, axis=0)
    parts = gather_tokens(tokens.reshape(n_tok, 2, 128).transpose(1, 0, 2))
    rows = weights[:, cols * 128, :cols].astype(jnp.int32)
    away = (lax.axis_index("z") - rows % 32 // 2) % 16
    rows = away * 4 + (rows // 32 + lax.axis_index("yh")) % 2 * 2 + rows % 2
    activated, grad_hidden, grads = hidden_call(rows, parts, weights, grad_act)
    grads = lax.all_to_all(grads, SEQ, 0, 0)
    summed = reduce_terms(*term_call(rows, grad_hidden, weights))
    summed = summed.transpose(1, 0, 2).reshape(n_tok, 256)
    grads = total(*grads).astype(BF16).transpose(0, 2, 1)
    return activated, summed, grads[:, None]


def solution(mesh):
    fine = Mesh(mesh.devices.reshape(SIZES), AXES)
    in_specs = (P(SEQ, MP), P(MP, SEQ, None, None), P(MP, SEQ), P(SEQ, MP))
    out_specs = (P(SEQ, MP), P(SEQ, MP), P(MP, SEQ, None, None))
    return jax.shard_map(shards, mesh=fine, in_specs=in_specs, out_specs=out_specs, check_vma=False)
```

```python
import jax
import jax.numpy as jnp
from jax import lax
from jax.experimental import pallas as pl
from jax.experimental.pallas import tpu as pltpu
from jax.sharding import Mesh
from jax.sharding import PartitionSpec as P

SQRT_TWO_PI = 0.7978845608028654
CUBIC = 0.044715
AXES = ("x", "yl", "core", "yh", "zh", "zl")
SIZES = (4, 2, 2, 2, 4, 4)
SEQ = ("x", "yl", "core")
FAR = ("yh", "zh")
MP = ("yh", "zh", "zl")
Z = ("zh", "zl")
BF16, F32 = jnp.bfloat16, jnp.float32
OWN, RIGHT, FAR_LEFT, FAR_RIGHT, LEFT = (0, 16), (16, 16), (32, 8), (40, 8), (48, 16)
PARTS = (OWN, LEFT, RIGHT, FAR_LEFT, FAR_RIGHT)


def gelu_parts(hidden):
    inner_arg = SQRT_TWO_PI * (hidden + CUBIC * hidden * hidden * hidden)
    tanh_inner = jnp.tanh(inner_arg)
    gelu_value = 0.5 * hidden * (1.0 + tanh_inner)
    gelu_slope = 0.5 * (1.0 + tanh_inner) + 0.5 * hidden * (
        1.0 - tanh_inner * tanh_inner
    ) * SQRT_TWO_PI * (1.0 + 3.0 * CUBIC * hidden * hidden)
    return gelu_value, gelu_slope


def fetch_columns(w_ref, w_all, w_sem):
    for c in range(w_ref.shape[1] // 128):
        own = (slice(None), slice(c * 128, (c + 1) * 128))
        pltpu.make_async_copy(w_ref.at[own], w_all.at[:, c], w_sem.at[c]).start()


def await_column(w_ref, w_all, w_sem, c):
    pltpu.make_async_copy(w_ref.at[:, pl.ds(0, 128)], w_all.at[:, c], w_sem.at[c]).wait()


def hidden_kernel(
    rows_ref, core_ref, own, left, right, far_left, far_right, w_ref, gact_ref, act_ref, gh_ref, keep_ref, give_ref, tok, w_all, sem, w_sem
):
    c = pl.program_id(0)
    half = keep_ref.shape[0]

    @pl.when(c == 0)
    def _():
        copies = [
            pltpu.make_async_copy(ref, tok.at[pl.ds(start, size)], sem.at[i])
            for i, (ref, (start, size)) in enumerate(zip((own, left, right, far_left, far_right), PARTS))
        ]
        for copy in copies:
            copy.start()
        fetch_columns(w_ref, w_all, w_sem)
        for copy in copies:
            copy.wait()

    await_column(w_ref, w_all, w_sem, c)
    core = core_ref[0]
    slots = [2 * j + core for j in range(half)] + [2 * j + 1 - core for j in range(half)]
    weights = jnp.concatenate([w_all[k, c] for k in slots], axis=0)
    picked = jnp.concatenate([tok[rows_ref[k, c]] for k in slots], axis=1)
    hidden = jnp.dot(picked, weights, preferred_element_type=F32)
    value, slope = gelu_parts(hidden)
    act_ref[...] = value.astype(BF16)
    grad_hidden = (gact_ref[...].astype(F32) * slope).astype(BF16)
    gh_ref[...] = grad_hidden
    grads = lax.dot_general(
        grad_hidden, picked, (((0,), (0,)), ((), ())), preferred_element_type=F32
    ).astype(BF16)
    for j in range(half):
        keep_ref[j, 0] = grads[:, j * 128 : (j + 1) * 128]
        give_ref[j, 0] = grads[:, (half + j) * 128 : (half + j + 1) * 128]


def term_kernel(rows_ref, gh_ref, w_ref, own, left, right, far_left, far_right, acc, w_all, w_sem):
    c = pl.program_id(0)
    kept = w_ref.shape[0]

    @pl.when(c == 0)
    def _():
        fetch_columns(w_ref, w_all, w_sem)
        acc[...] = jnp.zeros_like(acc)

    await_column(w_ref, w_all, w_sem, c)
    weights = jnp.concatenate([w_all[k, c] for k in range(kept)], axis=0)
    part = lax.dot_general(
        gh_ref[...], weights, (((1,), (1,)), ((), ())), preferred_element_type=F32
    )
    for k in range(kept):
        acc[rows_ref[k, c]] += part[:, k * 128 : (k + 1) * 128]

    @pl.when(c == pl.num_programs(0) - 1)
    def _():
        for ref, (start, size) in zip((own, left, right, far_left, far_right), PARTS):
            ref[...] = acc[start : start + size].astype(BF16)


def hidden_call(rows, core, parts, weights, grad_act):
    kept, cols = rows.shape
    n_tok = grad_act.shape[0]
    column = pl.BlockSpec((n_tok, 128), lambda c, *_: (0, c))
    half = pl.BlockSpec((kept // 2, 1, 128, 128), lambda c, *_: (0, c, 0, 0))
    wide = jax.ShapeDtypeStruct((n_tok, cols * 128), BF16)
    grads = jax.ShapeDtypeStruct((kept // 2, cols, 128, 128), BF16)
    return pl.pallas_call(
        hidden_kernel,
        grid_spec=pltpu.PrefetchScalarGridSpec(
            num_scalar_prefetch=2,
            grid=(cols,),
            in_specs=[pl.BlockSpec(memory_space=pl.ANY)] * 5
            + [pl.BlockSpec(memory_space=pltpu.HBM), column],
            out_specs=[column, column, half, half],
            scratch_shapes=[
                pltpu.VMEM((64, n_tok, 128), BF16),
                pltpu.VMEM((kept, cols, 128, 128), BF16),
                pltpu.SemaphoreType.DMA((5,)),
                pltpu.SemaphoreType.DMA((cols,)),
            ],
        ),
        out_shape=[wide, wide, grads, grads],
        compiler_params=pltpu.CompilerParams(vmem_limit_bytes=18 * 2**20),
        cost_estimate=pl.CostEstimate(flops=1_073_741_824, bytes_accessed=11_000_000, transcendentals=131072),
    )(rows, core, *parts, weights, grad_act)


def term_call(rows, grad_hidden, weights):
    kept, cols = rows.shape
    n_tok = grad_hidden.shape[0]
    return pl.pallas_call(
        term_kernel,
        grid_spec=pltpu.PrefetchScalarGridSpec(
            num_scalar_prefetch=1,
            grid=(cols,),
            in_specs=[
                pl.BlockSpec((n_tok, 128), lambda c, rows: (0, c)),
                pl.BlockSpec(memory_space=pltpu.HBM),
            ],
            out_specs=[pl.BlockSpec((n, n_tok, 128), lambda c, rows: (0, 0, 0)) for _, n in PARTS],
            scratch_shapes=[
                pltpu.VMEM((64, n_tok, 128), F32),
                pltpu.VMEM((kept, cols, 128, 128), BF16),
                pltpu.SemaphoreType.DMA((cols,)),
            ],
        ),
        out_shape=[jax.ShapeDtypeStruct((n, n_tok, 128), BF16) for _, n in PARTS],
        compiler_params=pltpu.CompilerParams(vmem_limit_bytes=20 * 2**20),
        cost_estimate=pl.CostEstimate(flops=536_870_912, bytes_accessed=7_000_000, transcendentals=0),
    )(rows, grad_hidden, weights)


def shift(a, by):
    return lax.ppermute(a, Z, [(i, (i + by) % 16) for i in range(16)])


def total(*arrays):
    return sum(a.astype(F32) for a in arrays)


def gather_tokens(mine):
    own = lax.all_to_all(jnp.broadcast_to(mine, (8,) + mine.shape), FAR, 0, 0)
    own = own.reshape((16,) + mine.shape[1:])
    left, right = shift(own, 1), shift(own, -1)
    return own, left, right, shift(left[:8], 1), shift(right[8:], -1)


def combine_kernel(own_ref, left_ref, right_ref, grads_ref, own_out, grads_out):
    own_out[...] = total(own_ref[...], left_ref[...], right_ref[...]).astype(BF16)
    for c in range(grads_ref.shape[1]):
        summed = sum(grads_ref[i, c].astype(F32) for i in range(grads_ref.shape[0]))
        grads_out[c] = summed.T.astype(BF16)


def add_kernel(keep_ref, got_ref, after_ref, both_ref):
    both_ref[...] = total(keep_ref[...], got_ref[...]).astype(BF16)


def add_after(keep, got, after):
    block = pl.BlockSpec((2,) + keep.shape[1:], lambda i: (i, 0, 0, 0))
    return pl.pallas_call(
        add_kernel,
        grid=(keep.shape[0] // 2,),
        in_specs=[block, block, pl.BlockSpec(memory_space=pl.ANY)],
        out_specs=block,
        out_shape=jax.ShapeDtypeStruct(keep.shape, BF16),
        compiler_params=pltpu.CompilerParams(vmem_limit_bytes=8 * 2**20),
        cost_estimate=pl.CostEstimate(flops=1_000_000, bytes_accessed=6_300_000, transcendentals=0),
    )(keep, got, after)


def reduce_all(keep, give, own, left, right, far_left, far_right):
    from_right, from_left = shift(far_left, -1), shift(far_right, 1)
    both = add_after(keep, lax.ppermute(give, "core", [(0, 1), (1, 0)]), own)
    grads = lax.all_to_all(both, ("x", "yl"), 0, 0)
    left = jnp.concatenate([total(left[:8], from_right).astype(BF16), left[8:]])
    right = jnp.concatenate([right[:8], total(right[8:], from_left).astype(BF16)])
    own, grads = pl.pallas_call(
        combine_kernel,
        out_shape=[
            jax.ShapeDtypeStruct(own.shape, BF16),
            jax.ShapeDtypeStruct(grads.shape[1:], BF16),
        ],
        compiler_params=pltpu.CompilerParams(vmem_limit_bytes=12 * 2**20),
        cost_estimate=pl.CostEstimate(flops=2_000_000, bytes_accessed=4_500_000, transcendentals=0),
    )(own, shift(left, -1), shift(right, 1), grads)
    own = lax.all_to_all(own.reshape((8, 2) + own.shape[1:]), FAR, 0, 0)
    return total(*own).astype(BF16), grads[:, None]


def shards(tokens, block_values, block_rows, grad_act):
    n_tok = tokens.shape[0]
    cols = block_values.shape[0]
    parts = gather_tokens(tokens.reshape(n_tok, 2, 128).transpose(1, 0, 2))
    row_tile = jnp.zeros((16, 128), BF16).at[0, :cols].set(block_rows[:, 0].astype(BF16))
    sent = jnp.concatenate([block_values.reshape(cols * 128, 128), row_tile])
    weights = lax.all_gather(sent, SEQ, axis=0)
    rows = weights[:, cols * 128, :cols].astype(jnp.int32)
    rows = (rows // 2 - lax.axis_index("zl")) % 4 * 16 + rows // 32 * 8 + rows % 32 // 8 * 2 + rows % 2
    core = lax.axis_index("core").reshape(1)
    activated, grad_hidden, keep, give = hidden_call(rows, core, parts, weights, grad_act)
    terms = term_call(rows, grad_hidden, weights)
    summed, grads = reduce_all(keep, give, *terms)
    return activated, summed.transpose(1, 0, 2).reshape(n_tok, 256), grads


def solution(mesh):
    fine = Mesh(mesh.devices.reshape(SIZES), AXES)
    in_specs = (P(SEQ, MP), P(MP, SEQ, None, None), P(MP, SEQ), P(SEQ, MP))
    out_specs = (P(SEQ, MP), P(SEQ, MP), P(MP, SEQ, None, None))
    return jax.shard_map(shards, mesh=fine, in_specs=in_specs, out_specs=out_specs, check_vma=False)
```

```python
import jax
import jax.numpy as jnp
from jax import lax
from jax.experimental import pallas as pl
from jax.experimental.pallas import tpu as pltpu
from jax.sharding import Mesh
from jax.sharding import PartitionSpec as P

SQRT_TWO_PI = 0.7978845608028654
CUBIC = 0.044715
AXES = ("x", "yl", "core", "yh", "z")
SIZES = (4, 2, 2, 2, 16)
SEQ = ("x", "yl", "core")
MP = ("yh", "z")
BF16, F32 = jnp.bfloat16, jnp.float32
OWN, LEFT, RIGHT = (0, 4, 8, 12), (1, 5, 9, 13), (15, 3, 7, 11)
FAR_LEFT, FAR_RIGHT = (6, 10), (14, 2)
PARTS = (OWN, LEFT, RIGHT, FAR_LEFT, FAR_RIGHT)


def gelu_parts(hidden):
    inner_arg = SQRT_TWO_PI * (hidden + CUBIC * hidden * hidden * hidden)
    tanh_inner = jnp.tanh(inner_arg)
    gelu_value = 0.5 * hidden * (1.0 + tanh_inner)
    gelu_slope = 0.5 * (1.0 + tanh_inner) + 0.5 * hidden * (
        1.0 - tanh_inner * tanh_inner
    ) * SQRT_TWO_PI * (1.0 + 3.0 * CUBIC * hidden * hidden)
    return gelu_value, gelu_slope


def fetch_columns(w_ref, w_all, w_sem):
    for c in range(w_ref.shape[1] // 128):
        own = (slice(None), slice(c * 128, (c + 1) * 128))
        pltpu.make_async_copy(w_ref.at[own], w_all.at[:, c], w_sem.at[c]).start()


def await_column(w_ref, w_all, w_sem, c):
    pltpu.make_async_copy(w_ref.at[:, pl.ds(0, 128)], w_all.at[:, c], w_sem.at[c]).wait()


def hidden_kernel(
    rows_ref, core_ref, own, left, right, far_left, far_right, w_ref, gact_ref, act_ref, gh_ref, keep_ref, give_ref, tok, w_all, sem, w_sem
):
    c = pl.program_id(0)
    half = keep_ref.shape[0]

    @pl.when(c == 0)
    def _():
        copies = [
            pltpu.make_async_copy(ref.at[pl.ds(4 * i, 4)], tok.at[pl.ds(4 * d, 4)], sem.at[d])
            for ref, part in zip((own, left, right, far_left, far_right), PARTS)
            for i, d in enumerate(part)
        ]
        for copy in copies:
            copy.start()
        fetch_columns(w_ref, w_all, w_sem)
        for copy in copies:
            copy.wait()

    await_column(w_ref, w_all, w_sem, c)
    core = core_ref[0]
    slots = [2 * j + core for j in range(half)] + [2 * j + 1 - core for j in range(half)]
    weights = jnp.concatenate([w_all[k, c] for k in slots], axis=0)
    picked = jnp.concatenate([tok[rows_ref[k, c]] for k in slots], axis=1)
    hidden = jnp.dot(picked, weights, preferred_element_type=F32)
    value, slope = gelu_parts(hidden)
    act_ref[...] = value.astype(BF16)
    grad_hidden = (gact_ref[...].astype(F32) * slope).astype(BF16)
    gh_ref[...] = grad_hidden
    grads = lax.dot_general(
        grad_hidden, picked, (((0,), (0,)), ((), ())), preferred_element_type=F32
    ).astype(BF16)
    for j in range(half):
        keep_ref[j, 0] = grads[:, j * 128 : (j + 1) * 128]
        give_ref[j, 0] = grads[:, (half + j) * 128 : (half + j + 1) * 128]


def term_kernel(rows_ref, gh_ref, w_ref, own, left, right, far_left, far_right, acc, w_all, w_sem):
    c = pl.program_id(0)
    kept = w_ref.shape[0]

    @pl.when(c == 0)
    def _():
        fetch_columns(w_ref, w_all, w_sem)
        acc[...] = jnp.zeros_like(acc)

    await_column(w_ref, w_all, w_sem, c)
    weights = jnp.concatenate([w_all[k, c] for k in range(kept)], axis=0)
    part = lax.dot_general(
        gh_ref[...], weights, (((1,), (1,)), ((), ())), preferred_element_type=F32
    )
    for k in range(kept):
        acc[rows_ref[k, c]] += part[:, k * 128 : (k + 1) * 128]

    @pl.when(c == pl.num_programs(0) - 1)
    def _():
        for ref, part in zip((own, left, right, far_left, far_right), PARTS):
            for i, d in enumerate(part):
                ref[4 * i : 4 * i + 4] = acc[4 * d : 4 * d + 4].astype(BF16)


def hidden_call(rows, core, parts, weights, grad_act):
    kept, cols = rows.shape
    n_tok = grad_act.shape[0]
    column = pl.BlockSpec((n_tok, 128), lambda c, *_: (0, c))
    half = pl.BlockSpec((kept // 2, 1, 128, 128), lambda c, *_: (0, c, 0, 0))
    wide = jax.ShapeDtypeStruct((n_tok, cols * 128), BF16)
    grads = jax.ShapeDtypeStruct((kept // 2, cols, 128, 128), BF16)
    return pl.pallas_call(
        hidden_kernel,
        grid_spec=pltpu.PrefetchScalarGridSpec(
            num_scalar_prefetch=2,
            grid=(cols,),
            in_specs=[pl.BlockSpec(memory_space=pl.ANY)] * 5
            + [pl.BlockSpec(memory_space=pltpu.HBM), column],
            out_specs=[column, column, half, half],
            scratch_shapes=[
                pltpu.VMEM((64, n_tok, 128), BF16),
                pltpu.VMEM((kept, cols, 128, 128), BF16),
                pltpu.SemaphoreType.DMA((16,)),
                pltpu.SemaphoreType.DMA((cols,)),
            ],
        ),
        out_shape=[wide, wide, grads, grads],
        compiler_params=pltpu.CompilerParams(vmem_limit_bytes=18 * 2**20),
        cost_estimate=pl.CostEstimate(flops=1_073_741_824, bytes_accessed=11_000_000, transcendentals=131072),
    )(rows, core, *parts, weights, grad_act)


def term_call(rows, grad_hidden, weights):
    kept, cols = rows.shape
    n_tok = grad_hidden.shape[0]
    return pl.pallas_call(
        term_kernel,
        grid_spec=pltpu.PrefetchScalarGridSpec(
            num_scalar_prefetch=1,
            grid=(cols,),
            in_specs=[
                pl.BlockSpec((n_tok, 128), lambda c, rows: (0, c)),
                pl.BlockSpec(memory_space=pltpu.HBM),
            ],
            out_specs=[pl.BlockSpec((4 * len(p), n_tok, 128), lambda c, rows: (0, 0, 0)) for p in PARTS],
            scratch_shapes=[
                pltpu.VMEM((64, n_tok, 128), F32),
                pltpu.VMEM((kept, cols, 128, 128), BF16),
                pltpu.SemaphoreType.DMA((cols,)),
            ],
        ),
        out_shape=[jax.ShapeDtypeStruct((4 * len(p), n_tok, 128), BF16) for p in PARTS],
        compiler_params=pltpu.CompilerParams(vmem_limit_bytes=20 * 2**20),
        cost_estimate=pl.CostEstimate(flops=536_870_912, bytes_accessed=7_000_000, transcendentals=0),
    )(rows, grad_hidden, weights)


def shift(a, by):
    return lax.ppermute(a, "z", [(i, (i + by) % 16) for i in range(16)])


def swap(a, axis):
    return lax.ppermute(a, axis, [(0, 1), (1, 0)])


def total(*arrays):
    return sum(a.astype(F32) for a in arrays)


def gather_tokens(mine):
    pair = jnp.concatenate([mine, swap(mine, "yh")])
    left, right = shift(pair, 4), shift(pair, -4)
    own = jnp.concatenate([pair, left, shift(left[:2], 4), shift(right[2:], -4), right])
    left, right = shift(own, 1), shift(own, -1)
    return own, left, right, shift(left[4:12], 1), shift(right[:8], -1)


def reduce_terms(own, left, right, far_left, far_right):
    from_right, from_left = shift(far_left, -1), shift(far_right, 1)
    left = jnp.concatenate([left[:4], total(left[4:12], from_right).astype(BF16), left[12:]])
    right = jnp.concatenate([total(right[:8], from_left).astype(BF16), right[8:]])
    own = total(own, shift(left, -1), shift(right, 1)).astype(BF16)
    from_right, from_left = shift(own[8:10], -4), shift(own[10:12], 4)
    left = jnp.concatenate([total(own[4:6], from_right).astype(BF16), own[6:8]])
    right = jnp.concatenate([own[12:14], total(own[14:16], from_left).astype(BF16)])
    pair = total(own[:4], shift(left, -4), shift(right, 4)).astype(BF16)
    return total(pair[:2], swap(pair[2:], "yh")).astype(BF16)


def add_kernel(keep_ref, got_ref, after_ref, both_ref):
    both_ref[...] = total(keep_ref[...], got_ref[...]).astype(BF16)


def add_after(keep, got, after):
    block = pl.BlockSpec((2,) + keep.shape[1:], lambda i: (i, 0, 0, 0))
    return pl.pallas_call(
        add_kernel,
        grid=(keep.shape[0] // 2,),
        in_specs=[block, block, pl.BlockSpec(memory_space=pl.ANY)],
        out_specs=block,
        out_shape=jax.ShapeDtypeStruct(keep.shape, BF16),
        compiler_params=pltpu.CompilerParams(vmem_limit_bytes=8 * 2**20),
        cost_estimate=pl.CostEstimate(flops=1_000_000, bytes_accessed=6_300_000, transcendentals=0),
    )(keep, got, after)


def sum_kernel(grads_ref, out_ref):
    for c in range(grads_ref.shape[1]):
        summed = sum(grads_ref[i, c].astype(F32) for i in range(grads_ref.shape[0]))
        out_ref[c] = summed.T.astype(BF16)


def reduce_grads(keep, give, after):
    both = add_after(keep, swap(give, "core"), after)
    grads = lax.all_to_all(both, ("x", "yl"), 0, 0)
    return pl.pallas_call(
        sum_kernel,
        out_shape=jax.ShapeDtypeStruct(grads.shape[1:], BF16),
        compiler_params=pltpu.CompilerParams(vmem_limit_bytes=8 * 2**20),
        cost_estimate=pl.CostEstimate(flops=2_000_000, bytes_accessed=2_500_000, transcendentals=0),
    )(grads)[:, None]


def shards(tokens, block_values, block_rows, grad_act):
    n_tok = tokens.shape[0]
    cols = block_values.shape[0]
    parts = gather_tokens(tokens.reshape(n_tok, 2, 128).transpose(1, 0, 2))
    row_tile = jnp.zeros((16, 128), BF16).at[0, :cols].set(block_rows[:, 0].astype(BF16))
    sent = jnp.concatenate([block_values.reshape(cols * 128, 128), row_tile])
    weights = lax.all_gather(sent, SEQ, axis=0)
    rows = weights[:, cols * 128, :cols].astype(jnp.int32)
    away = (lax.axis_index("z") - rows % 32 // 2) % 16
    rows = away * 4 + (rows // 32 + lax.axis_index("yh")) % 2 * 2 + rows % 2
    core = lax.axis_index("core").reshape(1)
    activated, grad_hidden, keep, give = hidden_call(rows, core, parts, weights, grad_act)
    terms = term_call(rows, grad_hidden, weights)
    grads = reduce_grads(keep, give, terms[0])
    summed = reduce_terms(*terms)
    return activated, summed.transpose(1, 0, 2).reshape(n_tok, 256), grads


def solution(mesh):
    fine = Mesh(mesh.devices.reshape(SIZES), AXES)
    in_specs = (P(SEQ, MP), P(MP, SEQ, None, None), P(MP, SEQ), P(SEQ, MP))
    out_specs = (P(SEQ, MP), P(SEQ, MP), P(MP, SEQ, None, None))
    return jax.shard_map(shards, mesh=fine, in_specs=in_specs, out_specs=out_specs, check_vma=False)
```

```python
import jax
import jax.numpy as jnp
from jax import lax
from jax.experimental import pallas as pl
from jax.experimental.pallas import tpu as pltpu
from jax.sharding import Mesh
from jax.sharding import PartitionSpec as P

SQRT_TWO_PI = 0.7978845608028654
CUBIC = 0.044715
AXES = ("x", "yl", "core", "yh", "zh", "zl")
SIZES = (4, 2, 2, 2, 4, 4)
SEQ = ("x", "yl", "core")
MP = ("yh", "zh", "zl")
FAR = ("yh", "zh")
Z = ("zh", "zl")
BF16, F32 = jnp.bfloat16, jnp.float32
OWN, RIGHT, FAR_LEFT, FAR_RIGHT, LEFT = (0, 16), (16, 16), (32, 8), (40, 8), (48, 16)
PARTS = (OWN, LEFT, RIGHT, FAR_LEFT, FAR_RIGHT)


def gelu_parts(hidden):
    inner_arg = SQRT_TWO_PI * (hidden + CUBIC * hidden * hidden * hidden)
    tanh_inner = jnp.tanh(inner_arg)
    gelu_value = 0.5 * hidden * (1.0 + tanh_inner)
    gelu_slope = 0.5 * (1.0 + tanh_inner) + 0.5 * hidden * (
        1.0 - tanh_inner * tanh_inner
    ) * SQRT_TWO_PI * (1.0 + 3.0 * CUBIC * hidden * hidden)
    return gelu_value, gelu_slope


def fetch_columns(halves, w_all, w_sem):
    kept = halves[0].shape[0]
    for c in range(w_all.shape[1]):
        for h, w_ref in enumerate(halves):
            pltpu.make_async_copy(
                w_ref.at[:, pl.ds(c * 128, 128)], w_all.at[pl.ds(h * kept, kept), c], w_sem.at[c, h]
            ).start()


def await_column(halves, w_all, w_sem, c):
    kept = halves[0].shape[0]
    for h, w_ref in enumerate(halves):
        pltpu.make_async_copy(
            w_ref.at[:, pl.ds(0, 128)], w_all.at[pl.ds(h * kept, kept), c], w_sem.at[c, h]
        ).wait()


def hidden_kernel(
    rows_ref, own, left, right, far_left, far_right, mine, other, gact_ref, act_ref, gh_ref, keep_ref, give_ref, tok, w_all, sem, w_sem
):
    c = pl.program_id(0)
    half = keep_ref.shape[0]

    @pl.when(c == 0)
    def _():
        copies = [
            pltpu.make_async_copy(ref, tok.at[pl.ds(start, size)], sem.at[i])
            for i, (ref, (start, size)) in enumerate(zip((own, left, right, far_left, far_right), PARTS))
        ]
        for copy in copies:
            copy.start()
        fetch_columns((mine, other), w_all, w_sem)
        for copy in copies:
            copy.wait()

    await_column((mine, other), w_all, w_sem, c)
    weights = jnp.concatenate([w_all[k, c] for k in range(2 * half)], axis=0)
    picked = jnp.concatenate([tok[rows_ref[k, c]] for k in range(2 * half)], axis=1)
    hidden = jnp.dot(picked, weights, preferred_element_type=F32)
    value, slope = gelu_parts(hidden)
    act_ref[...] = value.astype(BF16)
    grad_hidden = (gact_ref[...].astype(F32) * slope).astype(BF16)
    gh_ref[...] = grad_hidden
    grads = lax.dot_general(
        grad_hidden, picked, (((0,), (0,)), ((), ())), preferred_element_type=F32
    ).astype(BF16)
    for j in range(half):
        keep_ref[j, 0] = grads[:, j * 128 : (j + 1) * 128]
        give_ref[j, 0] = grads[:, (half + j) * 128 : (half + j + 1) * 128]


def term_kernel(rows_ref, gh_ref, mine, other, own, left, right, far_left, far_right, acc, w_all, w_sem):
    c = pl.program_id(0)
    kept = w_all.shape[0]

    @pl.when(c == 0)
    def _():
        fetch_columns((mine, other), w_all, w_sem)
        acc[...] = jnp.zeros_like(acc)

    await_column((mine, other), w_all, w_sem, c)
    weights = jnp.concatenate([w_all[k, c] for k in range(kept)], axis=0)
    part = lax.dot_general(
        gh_ref[...], weights, (((1,), (1,)), ((), ())), preferred_element_type=F32
    )
    for k in range(kept):
        acc[rows_ref[k, c]] += part[:, k * 128 : (k + 1) * 128]

    @pl.when(c == pl.num_programs(0) - 1)
    def _():
        for ref, (start, size) in zip((own, left, right, far_left, far_right), PARTS):
            ref[...] = acc[start : start + size].astype(BF16)


def hidden_call(rows, parts, mine, other, grad_act):
    kept, cols = rows.shape
    n_tok = grad_act.shape[0]
    column = pl.BlockSpec((n_tok, 128), lambda c, *_: (0, c))
    half = pl.BlockSpec((kept // 2, 1, 128, 128), lambda c, *_: (0, c, 0, 0))
    wide = jax.ShapeDtypeStruct((n_tok, cols * 128), BF16)
    grads = jax.ShapeDtypeStruct((kept // 2, cols, 128, 128), BF16)
    return pl.pallas_call(
        hidden_kernel,
        grid_spec=pltpu.PrefetchScalarGridSpec(
            num_scalar_prefetch=1,
            grid=(cols,),
            in_specs=[pl.BlockSpec(memory_space=pl.ANY)] * 7 + [column],
            out_specs=[column, column, half, half],
            scratch_shapes=[
                pltpu.VMEM((64, n_tok, 128), BF16),
                pltpu.VMEM((kept, cols, 128, 128), BF16),
                pltpu.SemaphoreType.DMA((5,)),
                pltpu.SemaphoreType.DMA((cols, 2)),
            ],
        ),
        out_shape=[wide, wide, grads, grads],
        compiler_params=pltpu.CompilerParams(vmem_limit_bytes=18 * 2**20),
        cost_estimate=pl.CostEstimate(flops=1_073_741_824, bytes_accessed=11_000_000, transcendentals=131072),
    )(rows, *parts, mine, other, grad_act)


def term_call(rows, grad_hidden, mine, other):
    kept, cols = rows.shape
    n_tok = grad_hidden.shape[0]
    return pl.pallas_call(
        term_kernel,
        grid_spec=pltpu.PrefetchScalarGridSpec(
            num_scalar_prefetch=1,
            grid=(cols,),
            in_specs=[pl.BlockSpec((n_tok, 128), lambda c, rows: (0, c))]
            + [pl.BlockSpec(memory_space=pl.ANY)] * 2,
            out_specs=[pl.BlockSpec((n, n_tok, 128), lambda c, rows: (0, 0, 0)) for _, n in PARTS],
            scratch_shapes=[
                pltpu.VMEM((64, n_tok, 128), F32),
                pltpu.VMEM((kept, cols, 128, 128), BF16),
                pltpu.SemaphoreType.DMA((cols, 2)),
            ],
        ),
        out_shape=[jax.ShapeDtypeStruct((n, n_tok, 128), BF16) for _, n in PARTS],
        compiler_params=pltpu.CompilerParams(vmem_limit_bytes=20 * 2**20),
        cost_estimate=pl.CostEstimate(flops=536_870_912, bytes_accessed=7_000_000, transcendentals=0),
    )(rows, grad_hidden, mine, other)


def shift(a, by):
    return lax.ppermute(a, Z, [(i, (i + by) % 16) for i in range(16)])


def swap(a, axis):
    return lax.ppermute(a, axis, [(0, 1), (1, 0)])


def total(*arrays):
    return sum(a.astype(F32) for a in arrays)


def order_kernel(*refs):
    pass


def held_until(x, *after):
    anywhere = pl.BlockSpec(memory_space=pl.ANY)
    return pl.pallas_call(
        order_kernel,
        in_specs=[anywhere] * (1 + len(after)),
        out_specs=anywhere,
        out_shape=jax.ShapeDtypeStruct(x.shape, x.dtype),
        input_output_aliases={0: 0},
        compiler_params=pltpu.CompilerParams(vmem_limit_bytes=2**20),
    )(x, *after)


def gather_far(mine):
    own = lax.all_to_all(jnp.broadcast_to(mine, (8,) + mine.shape), FAR, 0, 0)
    return own.reshape((16,) + mine.shape[1:])


def gather_near(own):
    left, right = shift(own, 1), shift(own, -1)
    return own, left, right, shift(left[:8], 1), shift(right[8:], -1)


def near_kernel(left_ref, right_ref, from_right, from_left, left_out, right_out):
    left_out[...] = total(left_ref[...], from_right[...]).astype(BF16)
    right_out[...] = total(right_ref[...], from_left[...]).astype(BF16)


def add_near(left, right, from_right, from_left):
    n, n_tok, _ = left.shape
    first = pl.BlockSpec((n // 2, n_tok, 128), lambda i: (0, 0, 0))
    second = pl.BlockSpec((n // 2, n_tok, 128), lambda i: (1, 0, 0))
    return pl.pallas_call(
        near_kernel,
        grid=(1,),
        in_specs=[first, second, first, first],
        out_specs=[first, second],
        out_shape=[jax.ShapeDtypeStruct(left.shape, BF16)] * 2,
        input_output_aliases={0: 0, 1: 1},
        compiler_params=pltpu.CompilerParams(vmem_limit_bytes=6 * 2**20),
        cost_estimate=pl.CostEstimate(flops=500_000, bytes_accessed=1_500_000, transcendentals=0),
    )(left, right, from_right, from_left)


def combine_kernel(own_ref, left_ref, right_ref, grads_ref, own_out, grads_out):
    own_out[...] = total(own_ref[...], left_ref[...], right_ref[...]).astype(BF16)
    for c in range(grads_ref.shape[1]):
        summed = sum(grads_ref[i, c].astype(F32) for i in range(grads_ref.shape[0]))
        grads_out[c] = summed.T.astype(BF16)


def finish_kernel(far_ref, out_ref):
    summed = sum(far_ref[i].astype(F32) for i in range(far_ref.shape[0])).astype(BF16)
    out_ref[...] = jnp.concatenate([summed[0], summed[1]], axis=1)


def reduce_all(keep, give, own, left, right, far_left, far_right):
    both = add_after(keep, swap(give, "core"), own)
    grads = lax.all_to_all(both, ("x", "yl"), 0, 0)
    left, right = add_near(left, right, shift(far_left, -1), shift(far_right, 1))
    own, grads = pl.pallas_call(
        combine_kernel,
        out_shape=[
            jax.ShapeDtypeStruct(own.shape, BF16),
            jax.ShapeDtypeStruct(grads.shape[1:], BF16),
        ],
        compiler_params=pltpu.CompilerParams(vmem_limit_bytes=12 * 2**20),
        cost_estimate=pl.CostEstimate(flops=2_000_000, bytes_accessed=4_500_000, transcendentals=0),
    )(own, shift(left, -1), shift(right, 1), grads)
    far = lax.all_to_all(own.reshape((8, 2) + own.shape[1:]), FAR, 0, 0)
    summed = pl.pallas_call(
        finish_kernel,
        out_shape=jax.ShapeDtypeStruct((own.shape[1], 256), BF16),
        compiler_params=pltpu.CompilerParams(vmem_limit_bytes=4 * 2**20),
        cost_estimate=pl.CostEstimate(flops=300_000, bytes_accessed=600_000, transcendentals=0),
    )(far)
    return summed, grads[:, None]


def order_kernel(*refs):
    pass


def held_until(x, *after):
    anywhere = pl.BlockSpec(memory_space=pl.ANY)
    return pl.pallas_call(
        order_kernel,
        in_specs=[anywhere] * (1 + len(after)),
        out_specs=anywhere,
        out_shape=jax.ShapeDtypeStruct(x.shape, x.dtype),
        input_output_aliases={0: 0},
        compiler_params=pltpu.CompilerParams(vmem_limit_bytes=2**20),
    )(x, *after)


def add_kernel(keep_ref, got_ref, after_ref, both_ref):
    both_ref[...] = total(keep_ref[...], got_ref[...]).astype(BF16)


def add_after(keep, got, after):
    block = pl.BlockSpec((2,) + keep.shape[1:], lambda i: (i, 0, 0, 0))
    return pl.pallas_call(
        add_kernel,
        grid=(keep.shape[0] // 2,),
        in_specs=[block, block, pl.BlockSpec(memory_space=pl.ANY)],
        out_specs=block,
        out_shape=jax.ShapeDtypeStruct(keep.shape, BF16),
        compiler_params=pltpu.CompilerParams(vmem_limit_bytes=8 * 2**20),
        cost_estimate=pl.CostEstimate(flops=1_000_000, bytes_accessed=6_300_000, transcendentals=0),
    )(keep, got, after)


def gather_weights(block_values, block_rows, after, later):
    cols = block_values.shape[0]
    row_tile = jnp.zeros((16, 128), BF16).at[0, :cols].set(block_rows[:, 0].astype(BF16))
    sent = jnp.concatenate([block_values.reshape(cols * 128, 128), row_tile])
    sent = held_until(jnp.broadcast_to(sent, (8,) + sent.shape), after)
    mine = held_until(lax.all_to_all(sent, ("x", "yl"), 0, 0), *later)
    other = swap(mine, "core")
    rows = jnp.concatenate([mine[:, cols * 128, :cols], other[:, cols * 128, :cols]])
    return mine, other, rows.astype(jnp.int32)


def place_of(rows):
    return (rows // 2 - lax.axis_index("zl")) % 4 * 16 + rows // 32 * 8 + rows % 32 // 8 * 2 + rows % 2


def shards(tokens, block_values, block_rows, grad_act):
    n_tok = tokens.shape[0]
    own = gather_far(tokens.reshape(n_tok, 2, 128).transpose(1, 0, 2))
    parts = gather_near(own)
    mine, other, rows = gather_weights(block_values, block_rows, own, parts[3:])
    rows = place_of(rows)
    activated, grad_hidden, keep, give = hidden_call(rows, parts, mine, other, grad_act)
    terms = term_call(rows, grad_hidden, mine, other)
    summed, grads = reduce_all(keep, give, *terms)
    return activated, summed, grads


def solution(mesh):
    fine = Mesh(mesh.devices.reshape(SIZES), AXES)
    in_specs = (P(SEQ, MP), P(MP, SEQ, None, None), P(MP, SEQ), P(SEQ, MP))
    out_specs = (P(SEQ, MP), P(SEQ, MP), P(MP, SEQ, None, None))
    return jax.shard_map(shards, mesh=fine, in_specs=in_specs, out_specs=out_specs, check_vma=False)
```

```python
import jax
import jax.numpy as jnp
from jax import lax
from jax.experimental import pallas as pl
from jax.experimental.pallas import tpu as pltpu
from jax.sharding import Mesh
from jax.sharding import PartitionSpec as P

SQRT_TWO_PI = 0.7978845608028654
CUBIC = 0.044715
AXES = ("x", "yl", "core", "yh", "zh", "zl")
SIZES = (4, 2, 2, 2, 4, 4)
SEQ = ("x", "yl", "core")
MP = ("yh", "zh", "zl")
FAR = ("yh", "zh")
Z = ("zh", "zl")
BF16, F32 = jnp.bfloat16, jnp.float32
OWN, RIGHT, FAR_LEFT, FAR_RIGHT, LEFT = (0, 16), (16, 16), (32, 8), (40, 8), (48, 16)
PARTS = (OWN, LEFT, RIGHT, FAR_LEFT, FAR_RIGHT)


def gelu_parts(hidden):
    inner_arg = SQRT_TWO_PI * (hidden + CUBIC * hidden * hidden * hidden)
    tanh_inner = jnp.tanh(inner_arg)
    gelu_value = 0.5 * hidden * (1.0 + tanh_inner)
    gelu_slope = 0.5 * (1.0 + tanh_inner) + 0.5 * hidden * (
        1.0 - tanh_inner * tanh_inner
    ) * SQRT_TWO_PI * (1.0 + 3.0 * CUBIC * hidden * hidden)
    return gelu_value, gelu_slope


def fetch_columns(halves, w_all, w_sem):
    kept = halves[0].shape[0]
    for c in range(w_all.shape[1]):
        for h, w_ref in enumerate(halves):
            pltpu.make_async_copy(
                w_ref.at[:, pl.ds(c * 128, 128)], w_all.at[pl.ds(h * kept, kept), c], w_sem.at[c, h]
            ).start()


def await_column(halves, w_all, w_sem, c):
    kept = halves[0].shape[0]
    for h, w_ref in enumerate(halves):
        pltpu.make_async_copy(
            w_ref.at[:, pl.ds(0, 128)], w_all.at[pl.ds(h * kept, kept), c], w_sem.at[c, h]
        ).wait()


def hidden_kernel(
    rows_ref, own, left, right, far_left, far_right, mine, other, gact_ref, act_ref, gh_ref, keep_ref, give_ref, tok, w_all, sem, w_sem
):
    c = pl.program_id(0)
    half = keep_ref.shape[0]

    @pl.when(c == 0)
    def _():
        copies = [
            pltpu.make_async_copy(ref, tok.at[pl.ds(start, size)], sem.at[i])
            for i, (ref, (start, size)) in enumerate(zip((own, left, right, far_left, far_right), PARTS))
        ]
        for copy in copies:
            copy.start()
        fetch_columns((mine, other), w_all, w_sem)
        for copy in copies:
            copy.wait()

    await_column((mine, other), w_all, w_sem, c)
    weights = jnp.concatenate([w_all[k, c] for k in range(2 * half)], axis=0)
    picked = jnp.concatenate([tok[rows_ref[k, c]] for k in range(2 * half)], axis=1)
    hidden = jnp.dot(picked, weights, preferred_element_type=F32)
    value, slope = gelu_parts(hidden)
    act_ref[...] = value.astype(BF16)
    grad_hidden = (gact_ref[...].astype(F32) * slope).astype(BF16)
    gh_ref[...] = grad_hidden
    grads = lax.dot_general(
        grad_hidden, picked, (((0,), (0,)), ((), ())), preferred_element_type=F32
    ).astype(BF16)
    for j in range(half):
        keep_ref[j, 0] = grads[:, j * 128 : (j + 1) * 128]
        give_ref[j, 0] = grads[:, (half + j) * 128 : (half + j + 1) * 128]


def term_kernel(rows_ref, gh_ref, mine, other, own, left, right, far_left, far_right, acc, w_all, w_sem):
    c = pl.program_id(0)
    kept = w_all.shape[0]

    @pl.when(c == 0)
    def _():
        fetch_columns((mine, other), w_all, w_sem)
        acc[...] = jnp.zeros_like(acc)

    await_column((mine, other), w_all, w_sem, c)
    weights = jnp.concatenate([w_all[k, c] for k in range(kept)], axis=0)
    part = lax.dot_general(
        gh_ref[...], weights, (((1,), (1,)), ((), ())), preferred_element_type=F32
    )
    for k in range(kept):
        acc[rows_ref[k, c]] += part[:, k * 128 : (k + 1) * 128]

    @pl.when(c == pl.num_programs(0) - 1)
    def _():
        for ref, (start, size) in zip((own, left, right, far_left, far_right), PARTS):
            ref[...] = acc[start : start + size].astype(BF16)


def hidden_call(rows, parts, mine, other, grad_act):
    kept, cols = rows.shape
    n_tok = grad_act.shape[0]
    column = pl.BlockSpec((n_tok, 128), lambda c, *_: (0, c))
    half = pl.BlockSpec((kept // 2, 1, 128, 128), lambda c, *_: (0, c, 0, 0))
    wide = jax.ShapeDtypeStruct((n_tok, cols * 128), BF16)
    grads = jax.ShapeDtypeStruct((kept // 2, cols, 128, 128), BF16)
    return pl.pallas_call(
        hidden_kernel,
        grid_spec=pltpu.PrefetchScalarGridSpec(
            num_scalar_prefetch=1,
            grid=(cols,),
            in_specs=[pl.BlockSpec(memory_space=pl.ANY)] * 7 + [column],
            out_specs=[column, column, half, half],
            scratch_shapes=[
                pltpu.VMEM((64, n_tok, 128), BF16),
                pltpu.VMEM((kept, cols, 128, 128), BF16),
                pltpu.SemaphoreType.DMA((5,)),
                pltpu.SemaphoreType.DMA((cols, 2)),
            ],
        ),
        out_shape=[wide, wide, grads, grads],
        compiler_params=pltpu.CompilerParams(vmem_limit_bytes=18 * 2**20),
        cost_estimate=pl.CostEstimate(flops=1_073_741_824, bytes_accessed=11_000_000, transcendentals=131072),
    )(rows, *parts, mine, other, grad_act)


def term_call(rows, grad_hidden, mine, other):
    kept, cols = rows.shape
    n_tok = grad_hidden.shape[0]
    return pl.pallas_call(
        term_kernel,
        grid_spec=pltpu.PrefetchScalarGridSpec(
            num_scalar_prefetch=1,
            grid=(cols,),
            in_specs=[pl.BlockSpec((n_tok, 128), lambda c, rows: (0, c))]
            + [pl.BlockSpec(memory_space=pl.ANY)] * 2,
            out_specs=[pl.BlockSpec((n, n_tok, 128), lambda c, rows: (0, 0, 0)) for _, n in PARTS],
            scratch_shapes=[
                pltpu.VMEM((64, n_tok, 128), F32),
                pltpu.VMEM((kept, cols, 128, 128), BF16),
                pltpu.SemaphoreType.DMA((cols, 2)),
            ],
        ),
        out_shape=[jax.ShapeDtypeStruct((n, n_tok, 128), BF16) for _, n in PARTS],
        compiler_params=pltpu.CompilerParams(vmem_limit_bytes=20 * 2**20),
        cost_estimate=pl.CostEstimate(flops=536_870_912, bytes_accessed=7_000_000, transcendentals=0),
    )(rows, grad_hidden, mine, other)


def shift(a, by):
    return lax.ppermute(a, Z, [(i, (i + by) % 16) for i in range(16)])


def swap(a, axis):
    return lax.ppermute(a, axis, [(0, 1), (1, 0)])


def total(*arrays):
    return sum(a.astype(F32) for a in arrays)


def order_kernel(*refs):
    pass


def held_until(x, *after):
    anywhere = pl.BlockSpec(memory_space=pl.ANY)
    return pl.pallas_call(
        order_kernel,
        in_specs=[anywhere] * (1 + len(after)),
        out_specs=anywhere,
        out_shape=jax.ShapeDtypeStruct(x.shape, x.dtype),
        input_output_aliases={0: 0},
        compiler_params=pltpu.CompilerParams(vmem_limit_bytes=2**20),
    )(x, *after)


def gather_tokens(pair):
    left, right = shift(pair, 4), shift(pair, -4)
    own = jnp.concatenate([pair, left, shift(left[:2], 4), shift(right[2:], -4), right])
    left, right = shift(own, 1), shift(own, -1)
    return own, left, right, shift(left[4:12], 1), shift(right[:8], -1)


def near_kernel(left_ref, right_ref, from_right, from_left, left_out, right_out):
    left_out[...] = total(left_ref[...], from_right[...]).astype(BF16)
    right_out[...] = total(right_ref[...], from_left[...]).astype(BF16)


def add_near(left, right, from_right, from_left):
    n, n_tok, _ = left.shape
    first = pl.BlockSpec((n // 2, n_tok, 128), lambda i: (0, 0, 0))
    second = pl.BlockSpec((n // 2, n_tok, 128), lambda i: (1, 0, 0))
    return pl.pallas_call(
        near_kernel,
        grid=(1,),
        in_specs=[first, second, first, first],
        out_specs=[first, second],
        out_shape=[jax.ShapeDtypeStruct(left.shape, BF16)] * 2,
        input_output_aliases={0: 0, 1: 1},
        compiler_params=pltpu.CompilerParams(vmem_limit_bytes=6 * 2**20),
        cost_estimate=pl.CostEstimate(flops=500_000, bytes_accessed=1_500_000, transcendentals=0),
    )(left, right, from_right, from_left)


def combine_kernel(own_ref, left_ref, right_ref, grads_ref, own_out, grads_out):
    own_out[...] = total(own_ref[...], left_ref[...], right_ref[...]).astype(BF16)
    for c in range(grads_ref.shape[1]):
        summed = sum(grads_ref[i, c].astype(F32) for i in range(grads_ref.shape[0]))
        grads_out[c] = summed.T.astype(BF16)


def finish_kernel(far_ref, out_ref):
    summed = sum(far_ref[i].astype(F32) for i in range(far_ref.shape[0])).astype(BF16)
    out_ref[...] = jnp.concatenate([summed[0], summed[1]], axis=1)


def reduce_all(both, own, left, right, far_left, far_right):
    grads = lax.all_to_all(both, ("x", "yl"), 0, 0)
    left, right = add_near(left, right, shift(far_left, -1), shift(far_right, 1))
    own, grads = pl.pallas_call(
        combine_kernel,
        out_shape=[
            jax.ShapeDtypeStruct(own.shape, BF16),
            jax.ShapeDtypeStruct(grads.shape[1:], BF16),
        ],
        compiler_params=pltpu.CompilerParams(vmem_limit_bytes=12 * 2**20),
        cost_estimate=pl.CostEstimate(flops=2_000_000, bytes_accessed=4_500_000, transcendentals=0),
    )(own, shift(left, -1), shift(right, 1), grads)
    far = lax.all_to_all(own.reshape((8, 2) + own.shape[1:]), FAR, 0, 0)
    summed = pl.pallas_call(
        finish_kernel,
        out_shape=jax.ShapeDtypeStruct((own.shape[1], 256), BF16),
        compiler_params=pltpu.CompilerParams(vmem_limit_bytes=4 * 2**20),
        cost_estimate=pl.CostEstimate(flops=300_000, bytes_accessed=600_000, transcendentals=0),
    )(far)
    return summed, grads[:, None]


def order_kernel(*refs):
    pass


def held_until(x, *after):
    anywhere = pl.BlockSpec(memory_space=pl.ANY)
    return pl.pallas_call(
        order_kernel,
        in_specs=[anywhere] * (1 + len(after)),
        out_specs=anywhere,
        out_shape=jax.ShapeDtypeStruct(x.shape, x.dtype),
        input_output_aliases={0: 0},
        compiler_params=pltpu.CompilerParams(vmem_limit_bytes=2**20),
    )(x, *after)


def add_kernel(keep_ref, got_ref, both_ref, mark_ref):
    both_ref[...] = total(keep_ref[...], got_ref[...]).astype(BF16)
    mark_ref[...] = jnp.zeros_like(mark_ref)


def add_halves(keep, got):
    block = pl.BlockSpec((2,) + keep.shape[1:], lambda i: (i, 0, 0, 0))
    return pl.pallas_call(
        add_kernel,
        grid=(keep.shape[0] // 2,),
        in_specs=[block, block],
        out_specs=[block, pl.BlockSpec((8, 128), lambda i: (0, 0))],
        out_shape=[
            jax.ShapeDtypeStruct(keep.shape, BF16),
            jax.ShapeDtypeStruct((8, 128), F32),
        ],
        compiler_params=pltpu.CompilerParams(vmem_limit_bytes=8 * 2**20),
        cost_estimate=pl.CostEstimate(flops=1_000_000, bytes_accessed=6_300_000, transcendentals=0),
    )(keep, got)


def gather_weights(block_values, block_rows, after, later):
    cols = block_values.shape[0]
    row_tile = jnp.zeros((16, 128), BF16).at[0, :cols].set(block_rows[:, 0].astype(BF16))
    sent = held_until(jnp.concatenate([block_values.reshape(cols * 128, 128), row_tile]), after)
    mine = lax.all_to_all(jnp.broadcast_to(sent, (8,) + sent.shape), ("x", "yl"), 0, 0)
    mine = held_until(mine, later)
    other = swap(mine, "core")
    rows = jnp.concatenate([mine[:, cols * 128, :cols], other[:, cols * 128, :cols]])
    return mine, other, rows.astype(jnp.int32)


def token_places(rows):
    z = lax.axis_index("zh") * 4 + lax.axis_index("zl")
    away = (z - rows % 32 // 2) % 16
    kind = away % 4
    group = jnp.where(kind == 0, 0, jnp.where(kind == 1, 48, jnp.where(kind == 2, 32, 16)))
    ahead = jnp.where(kind == 2, 10, jnp.where(kind == 3, 1, 0))
    other_yh = (rows // 32 + lax.axis_index("yh")) % 2
    return group + (away + ahead) // 4 % 4 * 4 + other_yh * 2 + rows % 2


def term_places(rows):
    return (rows // 2 - lax.axis_index("zl")) % 4 * 16 + rows // 32 * 8 + rows % 32 // 8 * 2 + rows % 2


def shards(tokens, block_values, block_rows, grad_act):
    n_tok = tokens.shape[0]
    mine = tokens.reshape(n_tok, 2, 128).transpose(1, 0, 2)
    pair = jnp.concatenate([mine, swap(mine, "yh")])
    parts = gather_tokens(pair)
    mine, other, rows = gather_weights(block_values, block_rows, pair, parts[0])
    activated, grad_hidden, keep, give = hidden_call(token_places(rows), parts, mine, other, grad_act)
    both, mark = add_halves(keep, swap(give, "core"))
    terms = term_call(term_places(rows), held_until(grad_hidden, mark), mine, other)
    summed, grads = reduce_all(both, *terms)
    return activated, summed, grads


def solution(mesh):
    fine = Mesh(mesh.devices.reshape(SIZES), AXES)
    in_specs = (P(SEQ, MP), P(MP, SEQ, None, None), P(MP, SEQ), P(SEQ, MP))
    out_specs = (P(SEQ, MP), P(SEQ, MP), P(MP, SEQ, None, None))
    return jax.shard_map(shards, mesh=fine, in_specs=in_specs, out_specs=out_specs, check_vma=False)
```

```python
import jax
import jax.numpy as jnp
from jax import lax
from jax.experimental import pallas as pl
from jax.experimental.pallas import tpu as pltpu
from jax.sharding import Mesh
from jax.sharding import PartitionSpec as P

SQRT_TWO_PI = 0.7978845608028654
CUBIC = 0.044715
AXES = ("x", "yl", "core", "yh", "z")
SIZES = (4, 2, 2, 2, 16)
SEQ = ("x", "yl", "core")
MP = ("yh", "z")
RING = 16
BF16, F32 = jnp.bfloat16, jnp.float32


def gelu_parts(hidden):
    inner_arg = SQRT_TWO_PI * (hidden + CUBIC * hidden * hidden * hidden)
    tanh_inner = jnp.tanh(inner_arg)
    gelu_value = 0.5 * hidden * (1.0 + tanh_inner)
    gelu_slope = 0.5 * (1.0 + tanh_inner) + 0.5 * hidden * (
        1.0 - tanh_inner * tanh_inner
    ) * SQRT_TWO_PI * (1.0 + 3.0 * CUBIC * hidden * hidden)
    return gelu_value, gelu_slope


def fetch_columns(halves, w_all, w_sem):
    kept = halves[0].shape[0]
    for c in range(w_all.shape[1]):
        for h, w_ref in enumerate(halves):
            pltpu.make_async_copy(
                w_ref.at[:, pl.ds(c * 128, 128)], w_all.at[pl.ds(h * kept, kept), c], w_sem.at[c, h]
            ).start()


def await_column(halves, w_all, w_sem, c):
    kept = halves[0].shape[0]
    for h, w_ref in enumerate(halves):
        pltpu.make_async_copy(
            w_ref.at[:, pl.ds(0, 128)], w_all.at[pl.ds(h * kept, kept), c], w_sem.at[c, h]
        ).wait()


def hidden_kernel(rows_ref, *refs):
    parts = refs[:RING]
    mine, other, gact_ref, act_ref, gh_ref, keep_ref, give_ref, tok, w_all, sem, w_sem = refs[RING:]
    c = pl.program_id(0)
    half = keep_ref.shape[0]

    @pl.when(c == 0)
    def _():
        copies = [
            pltpu.make_async_copy(ref, tok.at[pl.ds(4 * i, 4)], sem.at[i]) for i, ref in enumerate(parts)
        ]
        for copy in copies:
            copy.start()
        fetch_columns((mine, other), w_all, w_sem)
        for copy in copies:
            copy.wait()

    await_column((mine, other), w_all, w_sem, c)
    weights = jnp.concatenate([w_all[k, c] for k in range(2 * half)], axis=0)
    picked = jnp.concatenate([tok[rows_ref[k, c]] for k in range(2 * half)], axis=1)
    hidden = jnp.dot(picked, weights, preferred_element_type=F32)
    value, slope = gelu_parts(hidden)
    act_ref[...] = value.astype(BF16)
    grad_hidden = (gact_ref[...].astype(F32) * slope).astype(BF16)
    gh_ref[...] = grad_hidden
    grads = lax.dot_general(
        grad_hidden, picked, (((0,), (0,)), ((), ())), preferred_element_type=F32
    ).astype(BF16)
    for j in range(half):
        keep_ref[j, 0] = grads[:, j * 128 : (j + 1) * 128]
        give_ref[j, 0] = grads[:, (half + j) * 128 : (half + j + 1) * 128]


def term_kernel(rows_ref, gh_ref, mine, other, *refs):
    acc, w_all, w_sem = refs[RING:]
    c = pl.program_id(0)
    kept = w_all.shape[0]

    @pl.when(c == 0)
    def _():
        fetch_columns((mine, other), w_all, w_sem)
        acc[...] = jnp.zeros_like(acc)

    await_column((mine, other), w_all, w_sem, c)
    weights = jnp.concatenate([w_all[k, c] for k in range(kept)], axis=0)
    part = lax.dot_general(
        gh_ref[...], weights, (((1,), (1,)), ((), ())), preferred_element_type=F32
    )
    for k in range(kept):
        acc[rows_ref[k, c]] += part[:, k * 128 : (k + 1) * 128]

    @pl.when(c == pl.num_programs(0) - 1)
    def _():
        for i, ref in enumerate(refs[:RING]):
            ref[...] = acc[4 * i : 4 * i + 4].astype(BF16)


def hidden_call(rows, parts, mine, other, grad_act):
    kept, cols = rows.shape
    n_tok = grad_act.shape[0]
    column = pl.BlockSpec((n_tok, 128), lambda c, *_: (0, c))
    half = pl.BlockSpec((kept // 2, 1, 128, 128), lambda c, *_: (0, c, 0, 0))
    wide = jax.ShapeDtypeStruct((n_tok, cols * 128), BF16)
    grads = jax.ShapeDtypeStruct((kept // 2, cols, 128, 128), BF16)
    return pl.pallas_call(
        hidden_kernel,
        grid_spec=pltpu.PrefetchScalarGridSpec(
            num_scalar_prefetch=1,
            grid=(cols,),
            in_specs=[pl.BlockSpec(memory_space=pl.ANY)] * (RING + 2) + [column],
            out_specs=[column, column, half, half],
            scratch_shapes=[
                pltpu.VMEM((64, n_tok, 128), BF16),
                pltpu.VMEM((kept, cols, 128, 128), BF16),
                pltpu.SemaphoreType.DMA((RING,)),
                pltpu.SemaphoreType.DMA((cols, 2)),
            ],
        ),
        out_shape=[wide, wide, grads, grads],
        compiler_params=pltpu.CompilerParams(vmem_limit_bytes=18 * 2**20),
        cost_estimate=pl.CostEstimate(flops=1_073_741_824, bytes_accessed=11_000_000, transcendentals=131072),
    )(rows, *parts, mine, other, grad_act)


def term_call(rows, grad_hidden, mine, other):
    kept, cols = rows.shape
    n_tok = grad_hidden.shape[0]
    return pl.pallas_call(
        term_kernel,
        grid_spec=pltpu.PrefetchScalarGridSpec(
            num_scalar_prefetch=1,
            grid=(cols,),
            in_specs=[pl.BlockSpec((n_tok, 128), lambda c, rows: (0, c))]
            + [pl.BlockSpec(memory_space=pl.ANY)] * 2,
            out_specs=[pl.BlockSpec((4, n_tok, 128), lambda c, rows: (0, 0, 0))] * RING,
            scratch_shapes=[
                pltpu.VMEM((64, n_tok, 128), F32),
                pltpu.VMEM((kept, cols, 128, 128), BF16),
                pltpu.SemaphoreType.DMA((cols, 2)),
            ],
        ),
        out_shape=[jax.ShapeDtypeStruct((4, n_tok, 128), BF16)] * RING,
        compiler_params=pltpu.CompilerParams(vmem_limit_bytes=20 * 2**20),
        cost_estimate=pl.CostEstimate(flops=536_870_912, bytes_accessed=7_000_000, transcendentals=0),
    )(rows, grad_hidden, mine, other)


def shift(a, by):
    return lax.ppermute(a, "z", [(i, (i + by) % RING) for i in range(RING)])


def swap(a, axis):
    return lax.ppermute(a, axis, [(0, 1), (1, 0)])


def total(*arrays):
    return sum(a.astype(F32) for a in arrays)


def gather_tokens(pair):
    parts = [pair] * RING
    up, down = pair, pair
    for step in range(1, RING // 2 + 1):
        got_up = shift(up, 1)
        if step < RING // 2:
            got_down = shift(down, -1)
            up = held_until(got_up, down)
            down = held_until(got_down, up)
            parts[step] = down
        else:
            up = got_up
        parts[-step] = up
    return parts


def step_kernel(got_ref, own_ref, after_ref, out_ref):
    out_ref[...] = total(got_ref[...], own_ref[...]).astype(BF16)


def add_step(got, own, after):
    block = pl.BlockSpec(memory_space=pltpu.VMEM)
    return pl.pallas_call(
        step_kernel,
        in_specs=[block, block, pl.BlockSpec(memory_space=pl.ANY)],
        out_specs=block,
        out_shape=jax.ShapeDtypeStruct(own.shape, BF16),
        compiler_params=pltpu.CompilerParams(vmem_limit_bytes=2 * 2**20),
        cost_estimate=pl.CostEstimate(flops=100_000, bytes_accessed=400_000, transcendentals=0),
    )(got, own, after)


def last_kernel(up_ref, down_ref, own_ref, keep_ref, give_ref):
    summed = total(up_ref[...], down_ref[...], own_ref[...])
    keep_ref[...] = summed[:2]
    give_ref[...] = summed[2:].astype(BF16)


def finish_kernel(keep_ref, got_ref, out_ref):
    summed = (keep_ref[...] + got_ref[...].astype(F32)).astype(BF16)
    out_ref[...] = jnp.concatenate([summed[0], summed[1]], axis=1)


def reduce_terms(terms):
    n_tok = terms[0].shape[1]
    half = RING // 2
    up, down = terms[half], terms[half + 1]
    for step in range(half - 1):
        got_up, got_down = shift(up, 1), shift(down, -1)
        up = add_step(got_up, terms[half - 1 - step], down)
        down = add_step(got_down, terms[half + 2 + step], up) if step < half - 2 else got_down
    keep, give = pl.pallas_call(
        last_kernel,
        out_shape=[
            jax.ShapeDtypeStruct((2, n_tok, 128), F32),
            jax.ShapeDtypeStruct((2, n_tok, 128), BF16),
        ],
        compiler_params=pltpu.CompilerParams(vmem_limit_bytes=4 * 2**20),
        cost_estimate=pl.CostEstimate(flops=200_000, bytes_accessed=600_000, transcendentals=0),
    )(shift(up, 1), down, terms[0])
    return pl.pallas_call(
        finish_kernel,
        out_shape=jax.ShapeDtypeStruct((n_tok, 256), BF16),
        compiler_params=pltpu.CompilerParams(vmem_limit_bytes=4 * 2**20),
        cost_estimate=pl.CostEstimate(flops=100_000, bytes_accessed=300_000, transcendentals=0),
    )(keep, swap(give, "yh"))


def sum_kernel(grads_ref, out_ref):
    for c in range(grads_ref.shape[1]):
        summed = sum(grads_ref[i, c].astype(F32) for i in range(grads_ref.shape[0]))
        out_ref[c] = summed.T.astype(BF16)


def sum_grads(grads):
    return pl.pallas_call(
        sum_kernel,
        out_shape=jax.ShapeDtypeStruct(grads.shape[1:], BF16),
        compiler_params=pltpu.CompilerParams(vmem_limit_bytes=8 * 2**20),
        cost_estimate=pl.CostEstimate(flops=2_000_000, bytes_accessed=2_500_000, transcendentals=0),
    )(grads)[:, None]


def order_kernel(*refs):
    pass


def held_until(x, *after):
    anywhere = pl.BlockSpec(memory_space=pl.ANY)
    return pl.pallas_call(
        order_kernel,
        in_specs=[anywhere] * (1 + len(after)),
        out_specs=anywhere,
        out_shape=jax.ShapeDtypeStruct(x.shape, x.dtype),
        input_output_aliases={0: 0},
        compiler_params=pltpu.CompilerParams(vmem_limit_bytes=2**20),
    )(x, *after)


def add_kernel(keep_ref, got_ref, both_ref, mark_ref):
    both_ref[...] = total(keep_ref[...], got_ref[...]).astype(BF16)
    mark_ref[...] = jnp.zeros_like(mark_ref)


def add_halves(keep, got):
    block = pl.BlockSpec((2,) + keep.shape[1:], lambda i: (i, 0, 0, 0))
    return pl.pallas_call(
        add_kernel,
        grid=(keep.shape[0] // 2,),
        in_specs=[block, block],
        out_specs=[block, pl.BlockSpec((8, 128), lambda i: (0, 0))],
        out_shape=[
            jax.ShapeDtypeStruct(keep.shape, BF16),
            jax.ShapeDtypeStruct((8, 128), F32),
        ],
        compiler_params=pltpu.CompilerParams(vmem_limit_bytes=8 * 2**20),
        cost_estimate=pl.CostEstimate(flops=1_000_000, bytes_accessed=6_300_000, transcendentals=0),
    )(keep, got)


def gather_weights(block_values, block_rows, after, later):
    cols = block_values.shape[0]
    row_tile = jnp.zeros((16, 128), BF16).at[0, :cols].set(block_rows[:, 0].astype(BF16))
    sent = held_until(jnp.concatenate([block_values.reshape(cols * 128, 128), row_tile]), after)
    mine = lax.all_to_all(jnp.broadcast_to(sent, (8,) + sent.shape), ("x", "yl"), 0, 0)
    mine = held_until(mine, later)
    other = swap(mine, "core")
    rows = jnp.concatenate([mine[:, cols * 128, :cols], other[:, cols * 128, :cols]])
    return mine, other, rows.astype(jnp.int32)


def places(rows):
    ahead = (rows % 32 // 2 - lax.axis_index("z")) % RING
    return ahead * 4 + (rows // 32 + lax.axis_index("yh")) % 2 * 2 + rows % 2


def shards(tokens, block_values, block_rows, grad_act):
    n_tok = tokens.shape[0]
    mine = tokens.reshape(n_tok, 2, 128).transpose(1, 0, 2)
    pair = jnp.concatenate([mine, swap(mine, "yh")])
    parts = gather_tokens(pair)
    mine, other, rows = gather_weights(block_values, block_rows, pair, parts[5])
    rows = places(rows)
    activated, grad_hidden, keep, give = hidden_call(rows, parts, mine, other, grad_act)
    both, mark = add_halves(keep, swap(give, "core"))
    terms = term_call(rows, held_until(grad_hidden, mark), mine, other)
    grads = sum_grads(lax.all_to_all(both, ("x", "yl"), 0, 0))
    return activated, reduce_terms(terms), grads


def solution(mesh):
    fine = Mesh(mesh.devices.reshape(SIZES), AXES)
    in_specs = (P(SEQ, MP), P(MP, SEQ, None, None), P(MP, SEQ), P(SEQ, MP))
    out_specs = (P(SEQ, MP), P(SEQ, MP), P(MP, SEQ, None, None))
    return jax.shard_map(shards, mesh=fine, in_specs=in_specs, out_specs=out_specs, check_vma=False)
```

```python
import jax
import jax.numpy as jnp
from jax import lax
from jax.experimental import pallas as pl
from jax.experimental.pallas import tpu as pltpu
from jax.sharding import Mesh
from jax.sharding import PartitionSpec as P

SQRT_TWO_PI = 0.7978845608028654
CUBIC = 0.044715
AXES = ("x", "yl", "core", "yh", "z")
SIZES = (4, 2, 2, 2, 16)
SEQ = ("x", "yl", "core")
MP = ("yh", "z")
RING = 16
HALF = RING // 2 + 1
BF16, F32 = jnp.bfloat16, jnp.float32


def gelu_parts(hidden):
    inner_arg = SQRT_TWO_PI * (hidden + CUBIC * hidden * hidden * hidden)
    tanh_inner = jnp.tanh(inner_arg)
    gelu_value = 0.5 * hidden * (1.0 + tanh_inner)
    gelu_slope = 0.5 * (1.0 + tanh_inner) + 0.5 * hidden * (
        1.0 - tanh_inner * tanh_inner
    ) * SQRT_TWO_PI * (1.0 + 3.0 * CUBIC * hidden * hidden)
    return gelu_value, gelu_slope


def fetch_columns(halves, w_all, w_sem):
    kept = halves[0].shape[0]
    for c in range(w_all.shape[1]):
        for h, w_ref in enumerate(halves):
            pltpu.make_async_copy(
                w_ref.at[:, pl.ds(c * 128, 128)], w_all.at[pl.ds(h * kept, kept), c], w_sem.at[c, h]
            ).start()


def await_column(halves, w_all, w_sem, c):
    kept = halves[0].shape[0]
    for h, w_ref in enumerate(halves):
        pltpu.make_async_copy(
            w_ref.at[:, pl.ds(0, 128)], w_all.at[pl.ds(h * kept, kept), c], w_sem.at[c, h]
        ).wait()


def hidden_kernel(rows_ref, *refs):
    parts, rest = refs[:HALF], refs[HALF]
    mine, other, gact_ref, act_ref, gh_ref, keep_ref, give_ref, tok, w_all, sem, w_sem = refs[HALF + 1 :]
    c = pl.program_id(0)
    half = keep_ref.shape[0]

    @pl.when(c == 0)
    def _():
        copies = [
            pltpu.make_async_copy(ref.at[0], tok.at[pl.ds(4 * i, 4)], sem.at[i])
            for i, ref in enumerate(parts)
        ]
        copies.append(pltpu.make_async_copy(rest, tok.at[pl.ds(4 * HALF, rest.shape[0])], sem.at[HALF]))
        for copy in copies:
            copy.start()
        fetch_columns((mine, other), w_all, w_sem)
        for copy in copies:
            copy.wait()

    await_column((mine, other), w_all, w_sem, c)
    weights = jnp.concatenate([w_all[k, c] for k in range(2 * half)], axis=0)
    picked = jnp.concatenate([tok[rows_ref[k, c]] for k in range(2 * half)], axis=1)
    hidden = jnp.dot(picked, weights, preferred_element_type=F32)
    value, slope = gelu_parts(hidden)
    act_ref[...] = value.astype(BF16)
    grad_hidden = (gact_ref[...].astype(F32) * slope).astype(BF16)
    gh_ref[...] = grad_hidden
    grads = lax.dot_general(
        grad_hidden, picked, (((0,), (0,)), ((), ())), preferred_element_type=F32
    ).astype(BF16)
    for j in range(half):
        keep_ref[j, 0] = grads[:, j * 128 : (j + 1) * 128]
        give_ref[j, 0] = grads[:, (half + j) * 128 : (half + j + 1) * 128]


def term_kernel(rows_ref, gh_ref, mine, other, *refs):
    acc, w_all, w_sem = refs[HALF + 1 :]
    c = pl.program_id(0)
    kept = w_all.shape[0]

    @pl.when(c == 0)
    def _():
        fetch_columns((mine, other), w_all, w_sem)
        acc[...] = jnp.zeros_like(acc)

    await_column((mine, other), w_all, w_sem, c)
    weights = jnp.concatenate([w_all[k, c] for k in range(kept)], axis=0)
    part = lax.dot_general(
        gh_ref[...], weights, (((1,), (1,)), ((), ())), preferred_element_type=F32
    )
    for k in range(kept):
        acc[rows_ref[k, c]] += part[:, k * 128 : (k + 1) * 128]

    @pl.when(c == pl.num_programs(0) - 1)
    def _():
        for i, ref in enumerate(refs[:HALF]):
            ref[...] = acc[4 * i : 4 * i + 4].astype(BF16)
        refs[HALF][...] = acc[4 * HALF :].astype(BF16)


def hidden_call(rows, parts, mine, other, grad_act):
    kept, cols = rows.shape
    n_tok = grad_act.shape[0]
    column = pl.BlockSpec((n_tok, 128), lambda c, *_: (0, c))
    half = pl.BlockSpec((kept // 2, 1, 128, 128), lambda c, *_: (0, c, 0, 0))
    wide = jax.ShapeDtypeStruct((n_tok, cols * 128), BF16)
    grads = jax.ShapeDtypeStruct((kept // 2, cols, 128, 128), BF16)
    return pl.pallas_call(
        hidden_kernel,
        grid_spec=pltpu.PrefetchScalarGridSpec(
            num_scalar_prefetch=1,
            grid=(cols,),
            in_specs=[pl.BlockSpec(memory_space=pl.ANY)] * (HALF + 3) + [column],
            out_specs=[column, column, half, half],
            scratch_shapes=[
                pltpu.VMEM((64, n_tok, 128), BF16),
                pltpu.VMEM((kept, cols, 128, 128), BF16),
                pltpu.SemaphoreType.DMA((HALF + 1,)),
                pltpu.SemaphoreType.DMA((cols, 2)),
            ],
        ),
        out_shape=[wide, wide, grads, grads],
        compiler_params=pltpu.CompilerParams(vmem_limit_bytes=18 * 2**20),
        cost_estimate=pl.CostEstimate(flops=1_073_741_824, bytes_accessed=11_000_000, transcendentals=131072),
    )(rows, *parts, mine, other, grad_act)


def term_call(rows, grad_hidden, mine, other):
    kept, cols = rows.shape
    n_tok = grad_hidden.shape[0]
    return pl.pallas_call(
        term_kernel,
        grid_spec=pltpu.PrefetchScalarGridSpec(
            num_scalar_prefetch=1,
            grid=(cols,),
            in_specs=[pl.BlockSpec((n_tok, 128), lambda c, rows: (0, c))]
            + [pl.BlockSpec(memory_space=pl.ANY)] * 2,
            out_specs=[pl.BlockSpec((n, n_tok, 128), lambda c, rows: (0, 0, 0)) for n in [4] * HALF + [4 * (RING - HALF)]],
            scratch_shapes=[
                pltpu.VMEM((64, n_tok, 128), F32),
                pltpu.VMEM((kept, cols, 128, 128), BF16),
                pltpu.SemaphoreType.DMA((cols, 2)),
            ],
        ),
        out_shape=[jax.ShapeDtypeStruct((n, n_tok, 128), BF16) for n in [4] * HALF + [4 * (RING - HALF)]],
        compiler_params=pltpu.CompilerParams(vmem_limit_bytes=20 * 2**20),
        cost_estimate=pl.CostEstimate(flops=536_870_912, bytes_accessed=7_000_000, transcendentals=0),
    )(rows, grad_hidden, mine, other)


def onward(a):
    up = [(z, (z + 1) % RING) for z in range(RING)]
    down = [(RING + z, RING + (z - 1) % RING) for z in range(RING)]
    return lax.ppermute(a, ("core", "z"), up + down)


def swap(a, axis):
    return lax.ppermute(a, axis, [(0, 1), (1, 0)])


def total(*arrays):
    return sum(a.astype(F32) for a in arrays)


def pack_kernel(*refs):
    sources, out_ref, sem = refs[:-2], refs[-2], refs[-1]
    copies = [
        pltpu.make_async_copy(ref.at[1], out_ref.at[pl.ds(4 * i, 4)], sem.at[i])
        for i, ref in enumerate(sources)
    ]
    for copy in copies:
        copy.start()
    for copy in copies:
        copy.wait()


def gather_tokens(pair):
    rounds = [jnp.stack([pair, swap(pair, "core")])]
    for _ in range(RING // 2):
        rounds.append(onward(rounds[-1]))
    passed = rounds[1 : RING // 2]
    anywhere = pl.BlockSpec(memory_space=pl.ANY)
    others = pl.pallas_call(
        pack_kernel,
        in_specs=[anywhere] * len(passed),
        out_specs=anywhere,
        out_shape=jax.ShapeDtypeStruct((4 * len(passed),) + pair.shape[1:], BF16),
        scratch_shapes=[pltpu.SemaphoreType.DMA((len(passed),))],
        compiler_params=pltpu.CompilerParams(vmem_limit_bytes=2**20),
        cost_estimate=pl.CostEstimate(flops=0, bytes_accessed=1_800_000, transcendentals=0),
    )(*passed)
    return rounds, swap(others, "core")


def first_kernel(came_ref, own_ref, other_ref, out_ref):
    out_ref[0] = total(came_ref[...], own_ref[...]).astype(BF16)
    out_ref[1] = other_ref[...]


def step_kernel(came_ref, own_ref, other_ref, out_ref):
    out_ref[0] = total(came_ref[0], own_ref[...]).astype(BF16)
    out_ref[1] = total(came_ref[1], other_ref[...]).astype(BF16)


def add_step(came, own, others, steps):
    block = pl.BlockSpec(own.shape, lambda i: (0, 0, 0))
    both = pl.BlockSpec((2,) + own.shape, lambda i: (0, 0, 0, 0))
    return pl.pallas_call(
        first_kernel if came.ndim == 3 else step_kernel,
        grid=(1,),
        in_specs=[
            block if came.ndim == 3 else both,
            block,
            pl.BlockSpec(own.shape, lambda i: (steps - 1, 0, 0)),
        ],
        out_specs=both,
        out_shape=jax.ShapeDtypeStruct((2,) + own.shape, BF16),
        compiler_params=pltpu.CompilerParams(vmem_limit_bytes=4 * 2**20),
        cost_estimate=pl.CostEstimate(flops=200_000, bytes_accessed=800_000, transcendentals=0),
    )(came, own, others)


def arrive_kernel(came_ref, own_ref, keep_ref, give_ref):
    keep_ref[...] = total(came_ref[0], own_ref[...])
    give_ref[...] = came_ref[1]


def split_kernel(keep_ref, got_ref, mine_ref, give_ref):
    summed = keep_ref[...] + got_ref[...].astype(F32)
    mine_ref[...] = summed[:2]
    give_ref[...] = summed[2:].astype(BF16)


def finish_kernel(keep_ref, got_ref, out_ref):
    summed = (keep_ref[...] + got_ref[...].astype(F32)).astype(BF16)
    out_ref[...] = jnp.concatenate([summed[0], summed[1]], axis=1)


def small_call(kernel, args, outs):
    return pl.pallas_call(
        kernel,
        out_shape=outs,
        compiler_params=pltpu.CompilerParams(vmem_limit_bytes=4 * 2**20),
        cost_estimate=pl.CostEstimate(flops=200_000, bytes_accessed=600_000, transcendentals=0),
    )(*args)


def reduce_terms(terms):
    n_tok = terms[0].shape[1]
    shape = lambda n, dtype: jax.ShapeDtypeStruct((n, n_tok, 128), dtype)
    others = swap(terms[-1], "core")
    sums = terms[RING // 2]
    for steps in range(RING // 2 - 1, 0, -1):
        sums = add_step(onward(sums), terms[steps], others, steps)
    keep, give = small_call(arrive_kernel, (onward(sums), terms[0]), [shape(4, F32), shape(4, BF16)])
    keep, give = small_call(split_kernel, (keep, swap(give, "core")), [shape(2, F32), shape(2, BF16)])
    return small_call(finish_kernel, (keep, swap(give, "yh")), jax.ShapeDtypeStruct((n_tok, 256), BF16))


def sum_kernel(grads_ref, out_ref):
    for c in range(grads_ref.shape[1]):
        summed = sum(grads_ref[i, c].astype(F32) for i in range(grads_ref.shape[0]))
        out_ref[c] = summed.T.astype(BF16)


def sum_grads(grads):
    return pl.pallas_call(
        sum_kernel,
        out_shape=jax.ShapeDtypeStruct(grads.shape[1:], BF16),
        compiler_params=pltpu.CompilerParams(vmem_limit_bytes=8 * 2**20),
        cost_estimate=pl.CostEstimate(flops=2_000_000, bytes_accessed=2_500_000, transcendentals=0),
    )(grads)[:, None]


def order_kernel(*refs):
    pass


def held_until(x, *after):
    anywhere = pl.BlockSpec(memory_space=pl.ANY)
    return pl.pallas_call(
        order_kernel,
        in_specs=[anywhere] * (1 + len(after)),
        out_specs=anywhere,
        out_shape=jax.ShapeDtypeStruct(x.shape, x.dtype),
        input_output_aliases={0: 0},
        compiler_params=pltpu.CompilerParams(vmem_limit_bytes=2**20),
    )(x, *after)


def add_kernel(keep_ref, got_ref, both_ref):
    both_ref[...] = total(keep_ref[...], got_ref[...]).astype(BF16)


def add_halves(keep, got):
    block = pl.BlockSpec((2,) + keep.shape[1:], lambda i: (i, 0, 0, 0))
    return pl.pallas_call(
        add_kernel,
        grid=(keep.shape[0] // 2,),
        in_specs=[block, block],
        out_specs=block,
        out_shape=jax.ShapeDtypeStruct(keep.shape, BF16),
        compiler_params=pltpu.CompilerParams(vmem_limit_bytes=8 * 2**20),
        cost_estimate=pl.CostEstimate(flops=1_000_000, bytes_accessed=6_300_000, transcendentals=0),
    )(keep, got)


def gather_weights(block_values, block_rows, after, later):
    cols = block_values.shape[0]
    row_tile = jnp.zeros((16, 128), BF16).at[0, :cols].set(block_rows[:, 0].astype(BF16))
    sent = held_until(jnp.concatenate([block_values.reshape(cols * 128, 128), row_tile]), after)
    mine = lax.all_to_all(jnp.broadcast_to(sent, (8,) + sent.shape), ("x", "yl"), 0, 0)
    mine = held_until(mine, later)
    other = swap(mine, "core")
    rows = jnp.concatenate([mine[:, cols * 128, :cols], other[:, cols * 128, :cols]])
    return mine, other, rows.astype(jnp.int32)


def places(rows, sign):
    way = sign * (1 - 2 * lax.axis_index("core"))
    steps = way * (rows % 32 // 2 - lax.axis_index("z")) % RING
    slot = jnp.where(steps < HALF, steps, RING + HALF - 1 - steps)
    return slot * 4 + (rows // 32 + lax.axis_index("yh")) % 2 * 2 + rows % 2


def shards(tokens, block_values, block_rows, grad_act):
    n_tok = tokens.shape[0]
    mine = tokens.reshape(n_tok, 2, 128).transpose(1, 0, 2)
    pair = jnp.concatenate([mine, swap(mine, "yh")])
    rounds, rest = gather_tokens(pair)
    mine, other, rows = gather_weights(block_values, block_rows, pair, rounds[5])
    activated, grad_hidden, keep, give = hidden_call(places(rows, -1), (*rounds, rest), mine, other, grad_act)
    terms = term_call(places(rows, 1), grad_hidden, mine, other)
    both = add_halves(keep, swap(give, "core"))
    grads = sum_grads(lax.all_to_all(both, ("x", "yl"), 0, 0))
    return activated, reduce_terms(terms), grads


def solution(mesh):
    fine = Mesh(mesh.devices.reshape(SIZES), AXES)
    in_specs = (P(SEQ, MP), P(MP, SEQ, None, None), P(MP, SEQ), P(SEQ, MP))
    out_specs = (P(SEQ, MP), P(SEQ, MP), P(MP, SEQ, None, None))
    return jax.shard_map(shards, mesh=fine, in_specs=in_specs, out_specs=out_specs, check_vma=False)
```

```python
import jax
import jax.numpy as jnp
from jax import lax
from jax.experimental import pallas as pl
from jax.experimental.pallas import tpu as pltpu
from jax.sharding import Mesh
from jax.sharding import PartitionSpec as P

SQRT_TWO_PI = 0.7978845608028654
CUBIC = 0.044715
AXES = ("x", "yl", "core", "yh", "zh", "zl")
SIZES = (4, 2, 2, 2, 4, 4)
SEQ = ("x", "yl", "core")
FAR = ("yh", "zh")
MP = ("yh", "zh", "zl")
Z = ("zh", "zl")
BF16, F32 = jnp.bfloat16, jnp.float32
OWN, RIGHT, FAR_LEFT, FAR_RIGHT, LEFT = (0, 16), (16, 16), (32, 8), (40, 8), (48, 16)
PARTS = (OWN, LEFT, RIGHT, FAR_LEFT, FAR_RIGHT)


def gelu_parts(hidden):
    inner_arg = SQRT_TWO_PI * (hidden + CUBIC * hidden * hidden * hidden)
    tanh_inner = jnp.tanh(inner_arg)
    gelu_value = 0.5 * hidden * (1.0 + tanh_inner)
    gelu_slope = 0.5 * (1.0 + tanh_inner) + 0.5 * hidden * (
        1.0 - tanh_inner * tanh_inner
    ) * SQRT_TWO_PI * (1.0 + 3.0 * CUBIC * hidden * hidden)
    return gelu_value, gelu_slope


def fetch_columns(w_ref, w_all, w_sem):
    for c in range(w_ref.shape[1] // 128):
        own = (slice(None), slice(c * 128, (c + 1) * 128))
        pltpu.make_async_copy(w_ref.at[own], w_all.at[:, c], w_sem.at[c]).start()


def await_column(w_ref, w_all, w_sem, c):
    pltpu.make_async_copy(w_ref.at[:, pl.ds(0, 128)], w_all.at[:, c], w_sem.at[c]).wait()


def hidden_kernel(
    rows_ref, own, left, right, far_left, far_right, w_ref, gact_ref, act_ref, gh_ref, gv_ref, tok, w_all, sem, w_sem
):
    c = pl.program_id(0)
    kept = gv_ref.shape[0]

    @pl.when(c == 0)
    def _():
        copies = [
            pltpu.make_async_copy(ref, tok.at[pl.ds(start, size)], sem.at[i])
            for i, (ref, (start, size)) in enumerate(zip((own, left, right, far_left, far_right), PARTS))
        ]
        for copy in copies:
            copy.start()
        fetch_columns(w_ref, w_all, w_sem)
        for copy in copies:
            copy.wait()

    await_column(w_ref, w_all, w_sem, c)
    weights = jnp.concatenate([w_all[k, c] for k in range(kept)], axis=0)
    picked = jnp.concatenate([tok[rows_ref[k, c]] for k in range(kept)], axis=1)
    hidden = jnp.dot(picked, weights, preferred_element_type=F32)
    value, slope = gelu_parts(hidden)
    act_ref[...] = value.astype(BF16)
    grad_hidden = (gact_ref[...].astype(F32) * slope).astype(BF16)
    gh_ref[...] = grad_hidden
    grads = lax.dot_general(
        grad_hidden, picked, (((0,), (0,)), ((), ())), preferred_element_type=F32
    ).astype(BF16)
    for k in range(kept):
        gv_ref[k, 0] = grads[:, k * 128 : (k + 1) * 128]


def term_kernel(rows_ref, gh_ref, w_ref, own, left, right, far_left, far_right, acc, w_all, w_sem):
    c = pl.program_id(0)
    kept = w_ref.shape[0]

    @pl.when(c == 0)
    def _():
        fetch_columns(w_ref, w_all, w_sem)
        acc[...] = jnp.zeros_like(acc)

    await_column(w_ref, w_all, w_sem, c)
    weights = jnp.concatenate([w_all[k, c] for k in range(kept)], axis=0)
    part = lax.dot_general(
        gh_ref[...], weights, (((1,), (1,)), ((), ())), preferred_element_type=F32
    )
    for k in range(kept):
        acc[rows_ref[k, c]] += part[:, k * 128 : (k + 1) * 128]

    @pl.when(c == pl.num_programs(0) - 1)
    def _():
        for ref, (start, size) in zip((own, left, right, far_left, far_right), PARTS):
            ref[...] = acc[start : start + size].astype(BF16)


def hidden_call(rows, parts, weights, grad_act):
    kept, cols = rows.shape
    n_tok = grad_act.shape[0]
    column = pl.BlockSpec((n_tok, 128), lambda c, *_: (0, c))
    all_slots = pl.BlockSpec((kept, 1, 128, 128), lambda c, *_: (0, c, 0, 0))
    wide = jax.ShapeDtypeStruct((n_tok, cols * 128), BF16)
    grads = jax.ShapeDtypeStruct((kept, cols, 128, 128), BF16)
    return pl.pallas_call(
        hidden_kernel,
        grid_spec=pltpu.PrefetchScalarGridSpec(
            num_scalar_prefetch=1,
            grid=(cols,),
            in_specs=[pl.BlockSpec(memory_space=pl.ANY)] * 5
            + [pl.BlockSpec(memory_space=pltpu.HBM), column],
            out_specs=[column, column, all_slots],
            scratch_shapes=[
                pltpu.VMEM((64, n_tok, 128), BF16),
                pltpu.VMEM((kept, cols, 128, 128), BF16),
                pltpu.SemaphoreType.DMA((5,)),
                pltpu.SemaphoreType.DMA((cols,)),
            ],
        ),
        out_shape=[wide, wide, grads],
        compiler_params=pltpu.CompilerParams(vmem_limit_bytes=18 * 2**20),
        cost_estimate=pl.CostEstimate(flops=1_073_741_824, bytes_accessed=11_000_000, transcendentals=131072),
    )(rows, *parts, weights, grad_act)


def term_call(rows, grad_hidden, weights):
    kept, cols = rows.shape
    n_tok = grad_hidden.shape[0]
    return pl.pallas_call(
        term_kernel,
        grid_spec=pltpu.PrefetchScalarGridSpec(
            num_scalar_prefetch=1,
            grid=(cols,),
            in_specs=[
                pl.BlockSpec((n_tok, 128), lambda c, rows: (0, c)),
                pl.BlockSpec(memory_space=pltpu.HBM),
            ],
            out_specs=[pl.BlockSpec((n, n_tok, 128), lambda c, rows: (0, 0, 0)) for _, n in PARTS],
            scratch_shapes=[
                pltpu.VMEM((64, n_tok, 128), F32),
                pltpu.VMEM((kept, cols, 128, 128), BF16),
                pltpu.SemaphoreType.DMA((cols,)),
            ],
        ),
        out_shape=[jax.ShapeDtypeStruct((n, n_tok, 128), BF16) for _, n in PARTS],
        compiler_params=pltpu.CompilerParams(vmem_limit_bytes=20 * 2**20),
        cost_estimate=pl.CostEstimate(flops=536_870_912, bytes_accessed=7_000_000, transcendentals=0),
    )(rows, grad_hidden, weights)


def shift(a, by):
    return lax.ppermute(a, Z, [(i, (i + by) % 16) for i in range(16)])


def total(*arrays):
    return sum(a.astype(F32) for a in arrays)


def gather_tokens(mine):
    own = lax.all_to_all(jnp.broadcast_to(mine, (8,) + mine.shape), FAR, 0, 0)
    own = own.reshape((16,) + mine.shape[1:])
    left, right = shift(own, 1), shift(own, -1)
    return own, left, right, shift(left[:8], 1), shift(right[8:], -1)


def near_kernel(left_ref, right_ref, from_right, from_left, left_out, right_out):
    left_out[...] = total(left_ref[...], from_right[...]).astype(BF16)
    right_out[...] = total(right_ref[...], from_left[...]).astype(BF16)


def add_near(left, right, from_right, from_left):
    n, n_tok, _ = left.shape
    first = pl.BlockSpec((n // 2, n_tok, 128), lambda i: (0, 0, 0))
    second = pl.BlockSpec((n // 2, n_tok, 128), lambda i: (1, 0, 0))
    return pl.pallas_call(
        near_kernel,
        grid=(1,),
        in_specs=[first, second, first, first],
        out_specs=[first, second],
        out_shape=[jax.ShapeDtypeStruct(left.shape, BF16)] * 2,
        input_output_aliases={0: 0, 1: 1},
        compiler_params=pltpu.CompilerParams(vmem_limit_bytes=6 * 2**20),
        cost_estimate=pl.CostEstimate(flops=500_000, bytes_accessed=1_500_000, transcendentals=0),
    )(left, right, from_right, from_left)


def own_kernel(own_ref, left_ref, right_ref, out_ref):
    out_ref[...] = total(own_ref[...], left_ref[...], right_ref[...]).astype(BF16)


def finish_kernel(far_ref, out_ref):
    summed = sum(far_ref[i].astype(F32) for i in range(far_ref.shape[0])).astype(BF16)
    out_ref[...] = jnp.concatenate([summed[0], summed[1]], axis=1)


def small_call(kernel, args, out):
    return pl.pallas_call(
        kernel,
        out_shape=out,
        compiler_params=pltpu.CompilerParams(vmem_limit_bytes=6 * 2**20),
        cost_estimate=pl.CostEstimate(flops=500_000, bytes_accessed=2_000_000, transcendentals=0),
    )(*args)


def reduce_terms(own, left, right, far_left, far_right):
    n_tok = own.shape[1]
    left, right = add_near(left, right, shift(far_left, -1), shift(far_right, 1))
    out = jax.ShapeDtypeStruct(own.shape, BF16)
    own = small_call(own_kernel, (own, shift(left, -1), shift(right, 1)), out)
    far = lax.all_to_all(own.reshape((8, 2, n_tok, 128)), FAR, 0, 0)
    return small_call(finish_kernel, (far,), jax.ShapeDtypeStruct((n_tok, 256), BF16))


def shards(tokens, block_values, block_rows, grad_act):
    n_tok = tokens.shape[0]
    cols = block_values.shape[0]
    parts = gather_tokens(tokens.reshape(n_tok, 2, 128).transpose(1, 0, 2))
    row_tile = jnp.zeros((16, 128), BF16).at[0, :cols].set(block_rows[:, 0].astype(BF16))
    sent = jnp.concatenate([block_values.reshape(cols * 128, 128), row_tile])
    weights = lax.all_gather(sent, SEQ, axis=0)
    rows = weights[:, cols * 128, :cols].astype(jnp.int32)
    rows = (rows // 2 - lax.axis_index("zl")) % 4 * 16 + rows // 32 * 8 + rows % 32 // 8 * 2 + rows % 2
    activated, grad_hidden, grads = hidden_call(rows, parts, weights, grad_act)
    grads = lax.psum_scatter(grads, SEQ, scatter_dimension=0)
    summed = reduce_terms(*term_call(rows, grad_hidden, weights))
    return activated, summed, grads.transpose(0, 2, 1)[:, None]


def solution(mesh):
    fine = Mesh(mesh.devices.reshape(SIZES), AXES)
    in_specs = (P(SEQ, MP), P(MP, SEQ, None, None), P(MP, SEQ), P(SEQ, MP))
    out_specs = (P(SEQ, MP), P(SEQ, MP), P(MP, SEQ, None, None))
    return jax.shard_map(shards, mesh=fine, in_specs=in_specs, out_specs=out_specs, check_vma=False)
```

```python
import jax
import jax.numpy as jnp
from jax import lax
from jax.experimental import pallas as pl
from jax.experimental.pallas import tpu as pltpu
from jax.sharding import Mesh
from jax.sharding import PartitionSpec as P

SQRT_TWO_PI = 0.7978845608028654
CUBIC = 0.044715
AXES = ("x", "yl", "core", "yh", "zh", "zl")
SIZES = (4, 2, 2, 2, 4, 4)
SEQ = ("x", "yl", "core")
FAR = ("yh", "zh")
MP = ("yh", "zh", "zl")
Z = ("zh", "zl")
BF16, F32 = jnp.bfloat16, jnp.float32
OWN, RIGHT, FAR_LEFT, FAR_RIGHT, LEFT = (0, 16), (16, 16), (32, 8), (40, 8), (48, 16)
PARTS = (OWN, LEFT, RIGHT, FAR_LEFT, FAR_RIGHT)


def gelu_parts(hidden):
    inner_arg = SQRT_TWO_PI * (hidden + CUBIC * hidden * hidden * hidden)
    tanh_inner = jnp.tanh(inner_arg)
    gelu_value = 0.5 * hidden * (1.0 + tanh_inner)
    gelu_slope = 0.5 * (1.0 + tanh_inner) + 0.5 * hidden * (
        1.0 - tanh_inner * tanh_inner
    ) * SQRT_TWO_PI * (1.0 + 3.0 * CUBIC * hidden * hidden)
    return gelu_value, gelu_slope


def fetch_columns(w_ref, w_all, w_sem):
    for c in range(w_ref.shape[1] // 128):
        own = (slice(None), slice(c * 128, (c + 1) * 128))
        pltpu.make_async_copy(w_ref.at[own], w_all.at[:, c], w_sem.at[c]).start()


def await_column(w_ref, w_all, w_sem, c):
    pltpu.make_async_copy(w_ref.at[:, pl.ds(0, 128)], w_all.at[:, c], w_sem.at[c]).wait()


def hidden_kernel(
    rows_ref, own, left, right, far_left, far_right, w_ref, gact_ref, act_ref, gh_ref, gv_ref, tok, w_all, sem, w_sem
):
    c = pl.program_id(0)
    kept = gv_ref.shape[0]

    @pl.when(c == 0)
    def _():
        copies = [
            pltpu.make_async_copy(ref, tok.at[pl.ds(start, size)], sem.at[i])
            for i, (ref, (start, size)) in enumerate(zip((own, left, right, far_left, far_right), PARTS))
        ]
        for copy in copies:
            copy.start()
        fetch_columns(w_ref, w_all, w_sem)
        for copy in copies:
            copy.wait()

    await_column(w_ref, w_all, w_sem, c)
    weights = jnp.concatenate([w_all[k, c] for k in range(kept)], axis=0)
    picked = jnp.concatenate([tok[rows_ref[k, c]] for k in range(kept)], axis=1)
    hidden = jnp.dot(picked, weights, preferred_element_type=F32)
    value, slope = gelu_parts(hidden)
    act_ref[...] = value.astype(BF16)
    grad_hidden = (gact_ref[...].astype(F32) * slope).astype(BF16)
    gh_ref[...] = grad_hidden
    grads = lax.dot_general(
        grad_hidden, picked, (((0,), (0,)), ((), ())), preferred_element_type=F32
    ).astype(BF16)
    for k in range(kept):
        gv_ref[k, 0] = grads[:, k * 128 : (k + 1) * 128]


def term_kernel(rows_ref, gh_ref, w_ref, own, left, right, far_left, far_right, acc, w_all, w_sem):
    c = pl.program_id(0)
    kept = w_ref.shape[0]

    @pl.when(c == 0)
    def _():
        fetch_columns(w_ref, w_all, w_sem)
        acc[...] = jnp.zeros_like(acc)

    await_column(w_ref, w_all, w_sem, c)
    weights = jnp.concatenate([w_all[k, c] for k in range(kept)], axis=0)
    part = lax.dot_general(
        gh_ref[...], weights, (((1,), (1,)), ((), ())), preferred_element_type=F32
    )
    for k in range(kept):
        acc[rows_ref[k, c]] += part[:, k * 128 : (k + 1) * 128]

    @pl.when(c == pl.num_programs(0) - 1)
    def _():
        for ref, (start, size) in zip((own, left, right, far_left, far_right), PARTS):
            ref[...] = acc[start : start + size].astype(BF16)


def hidden_call(rows, parts, weights, grad_act):
    kept, cols = rows.shape
    n_tok = grad_act.shape[0]
    column = pl.BlockSpec((n_tok, 128), lambda c, *_: (0, c))
    all_slots = pl.BlockSpec((kept, 1, 128, 128), lambda c, *_: (0, c, 0, 0))
    wide = jax.ShapeDtypeStruct((n_tok, cols * 128), BF16)
    grads = jax.ShapeDtypeStruct((kept, cols, 128, 128), BF16)
    return pl.pallas_call(
        hidden_kernel,
        grid_spec=pltpu.PrefetchScalarGridSpec(
            num_scalar_prefetch=1,
            grid=(cols,),
            in_specs=[pl.BlockSpec(memory_space=pl.ANY)] * 5
            + [pl.BlockSpec(memory_space=pltpu.HBM), column],
            out_specs=[column, column, all_slots],
            scratch_shapes=[
                pltpu.VMEM((64, n_tok, 128), BF16),
                pltpu.VMEM((kept, cols, 128, 128), BF16),
                pltpu.SemaphoreType.DMA((5,)),
                pltpu.SemaphoreType.DMA((cols,)),
            ],
        ),
        out_shape=[wide, wide, grads],
        compiler_params=pltpu.CompilerParams(vmem_limit_bytes=56 * 2**20),
        cost_estimate=pl.CostEstimate(flops=1_073_741_824, bytes_accessed=11_000_000, transcendentals=131072),
    )(rows, *parts, weights, grad_act)


def term_call(rows, grad_hidden, weights):
    kept, cols = rows.shape
    n_tok = grad_hidden.shape[0]
    return pl.pallas_call(
        term_kernel,
        grid_spec=pltpu.PrefetchScalarGridSpec(
            num_scalar_prefetch=1,
            grid=(cols,),
            in_specs=[
                pl.BlockSpec((n_tok, 128), lambda c, rows: (0, c)),
                pl.BlockSpec(memory_space=pltpu.HBM),
            ],
            out_specs=[pl.BlockSpec((n, n_tok, 128), lambda c, rows: (0, 0, 0)) for _, n in PARTS],
            scratch_shapes=[
                pltpu.VMEM((64, n_tok, 128), F32),
                pltpu.VMEM((kept, cols, 128, 128), BF16),
                pltpu.SemaphoreType.DMA((cols,)),
            ],
        ),
        out_shape=[jax.ShapeDtypeStruct((n, n_tok, 128), BF16) for _, n in PARTS],
        compiler_params=pltpu.CompilerParams(vmem_limit_bytes=56 * 2**20),
        cost_estimate=pl.CostEstimate(flops=536_870_912, bytes_accessed=7_000_000, transcendentals=0),
    )(rows, grad_hidden, weights)


def shift(a, by):
    return lax.ppermute(a, Z, [(i, (i + by) % 16) for i in range(16)])


def total(*arrays):
    return sum(a.astype(F32) for a in arrays)


def gather_tokens(mine):
    own = lax.all_to_all(jnp.broadcast_to(mine, (8,) + mine.shape), FAR, 0, 0)
    own = own.reshape((16,) + mine.shape[1:])
    left, right = shift(own, 1), shift(own, -1)
    return own, left, right, shift(left[:8], 1), shift(right[8:], -1)


def turn_kernel(grads_ref, out_ref):
    for c in range(grads_ref.shape[0]):
        out_ref[c] = grads_ref[c].T


def near_kernel(left_ref, right_ref, from_right, from_left, left_out, right_out):
    left_out[...] = total(left_ref[...], from_right[...]).astype(BF16)
    right_out[...] = total(right_ref[...], from_left[...]).astype(BF16)


def add_near(left, right, from_right, from_left):
    n, n_tok, _ = left.shape
    first = pl.BlockSpec((n // 2, n_tok, 128), lambda i: (0, 0, 0))
    second = pl.BlockSpec((n // 2, n_tok, 128), lambda i: (1, 0, 0))
    return pl.pallas_call(
        near_kernel,
        grid=(1,),
        in_specs=[first, second, first, first],
        out_specs=[first, second],
        out_shape=[jax.ShapeDtypeStruct(left.shape, BF16)] * 2,
        input_output_aliases={0: 0, 1: 1},
        compiler_params=pltpu.CompilerParams(vmem_limit_bytes=6 * 2**20),
        cost_estimate=pl.CostEstimate(flops=500_000, bytes_accessed=1_500_000, transcendentals=0),
    )(left, right, from_right, from_left)


def own_kernel(own_ref, left_ref, right_ref, out_ref):
    out_ref[...] = total(own_ref[...], left_ref[...], right_ref[...]).astype(BF16)


def finish_kernel(far_ref, out_ref):
    summed = sum(far_ref[i].astype(F32) for i in range(far_ref.shape[0])).astype(BF16)
    out_ref[...] = jnp.concatenate([summed[0], summed[1]], axis=1)


def small_call(kernel, args, out):
    return pl.pallas_call(
        kernel,
        out_shape=out,
        compiler_params=pltpu.CompilerParams(vmem_limit_bytes=6 * 2**20),
        cost_estimate=pl.CostEstimate(flops=500_000, bytes_accessed=2_000_000, transcendentals=0),
    )(*args)


def reduce_terms(own, left, right, far_left, far_right):
    n_tok = own.shape[1]
    left, right = add_near(left, right, shift(far_left, -1), shift(far_right, 1))
    out = jax.ShapeDtypeStruct(own.shape, BF16)
    own = small_call(own_kernel, (own, shift(left, -1), shift(right, 1)), out)
    far = lax.all_to_all(own.reshape((8, 2, n_tok, 128)), FAR, 0, 0)
    return small_call(finish_kernel, (far,), jax.ShapeDtypeStruct((n_tok, 256), BF16))


def shards(tokens, block_values, block_rows, grad_act):
    n_tok = tokens.shape[0]
    cols = block_values.shape[0]
    parts = gather_tokens(tokens.reshape(n_tok, 2, 128).transpose(1, 0, 2))
    row_tile = jnp.zeros((16, 128), BF16).at[0, :cols].set(block_rows[:, 0].astype(BF16))
    sent = jnp.concatenate([block_values.reshape(cols * 128, 128), row_tile])
    weights = lax.all_gather(sent, SEQ, axis=0)
    rows = weights[:, cols * 128, :cols].astype(jnp.int32)
    rows = (rows // 2 - lax.axis_index("zl")) % 4 * 16 + rows // 32 * 8 + rows % 32 // 8 * 2 + rows % 2
    activated, grad_hidden, grads = hidden_call(rows, parts, weights, grad_act)
    grads = lax.psum_scatter(grads, SEQ, scatter_dimension=0)
    summed = reduce_terms(*term_call(rows, grad_hidden, weights))
    grads = small_call(turn_kernel, (grads,), jax.ShapeDtypeStruct(grads.shape, BF16))
    return activated, summed, grads[:, None]


def solution(mesh):
    fine = Mesh(mesh.devices.reshape(SIZES), AXES)
    in_specs = (P(SEQ, MP), P(MP, SEQ, None, None), P(MP, SEQ), P(SEQ, MP))
    out_specs = (P(SEQ, MP), P(SEQ, MP), P(MP, SEQ, None, None))
    return jax.shard_map(shards, mesh=fine, in_specs=in_specs, out_specs=out_specs, check_vma=False)
```

```python
import jax
import jax.numpy as jnp
from jax import lax
from jax.experimental import pallas as pl
from jax.experimental.pallas import tpu as pltpu
from jax.sharding import Mesh
from jax.sharding import PartitionSpec as P

SQRT_TWO_PI = 0.7978845608028654
CUBIC = 0.044715
AXES = ("x", "yl", "core", "yh", "zh", "zl")
SIZES = (4, 2, 2, 2, 4, 4)
SEQ = ("x", "yl", "core")
FAR = ("zh", "yh")
MP = ("yh", "zh", "zl")
Z = ("zh", "zl")
BF16, F32 = jnp.bfloat16, jnp.float32
OWN, RIGHT, FAR_LEFT, FAR_RIGHT, LEFT = (0, 16), (16, 16), (32, 8), (40, 8), (48, 16)
PARTS = (OWN, LEFT, RIGHT, FAR_LEFT, FAR_RIGHT)


def gelu_parts(hidden):
    inner_arg = SQRT_TWO_PI * (hidden + CUBIC * hidden * hidden * hidden)
    tanh_inner = jnp.tanh(inner_arg)
    gelu_value = 0.5 * hidden * (1.0 + tanh_inner)
    gelu_slope = 0.5 * (1.0 + tanh_inner) + 0.5 * hidden * (
        1.0 - tanh_inner * tanh_inner
    ) * SQRT_TWO_PI * (1.0 + 3.0 * CUBIC * hidden * hidden)
    return gelu_value, gelu_slope


def fetch_columns(w_ref, w_all, w_sem):
    for c in range(w_ref.shape[1] // 128):
        own = (slice(None), slice(c * 128, (c + 1) * 128))
        pltpu.make_async_copy(w_ref.at[own], w_all.at[:, c], w_sem.at[c]).start()


def await_column(w_ref, w_all, w_sem, c):
    pltpu.make_async_copy(w_ref.at[:, pl.ds(0, 128)], w_all.at[:, c], w_sem.at[c]).wait()


def hidden_kernel(
    rows_ref, own, left, right, far_left, far_right, w_ref, gact_ref, act_ref, gh_ref, gv_ref, tok, w_all, sem, w_sem
):
    c = pl.program_id(0)
    kept = gv_ref.shape[0]

    @pl.when(c == 0)
    def _():
        copies = [
            pltpu.make_async_copy(ref, tok.at[pl.ds(start, size)], sem.at[i])
            for i, (ref, (start, size)) in enumerate(zip((own, left, right, far_left, far_right), PARTS))
        ]
        for copy in copies:
            copy.start()
        fetch_columns(w_ref, w_all, w_sem)
        for copy in copies:
            copy.wait()

    await_column(w_ref, w_all, w_sem, c)
    weights = jnp.concatenate([w_all[k, c] for k in range(kept)], axis=0)
    picked = jnp.concatenate([tok[rows_ref[k, c]] for k in range(kept)], axis=1)
    hidden = jnp.dot(picked, weights, preferred_element_type=F32)
    value, slope = gelu_parts(hidden)
    act_ref[...] = value.astype(BF16)
    grad_hidden = (gact_ref[...].astype(F32) * slope).astype(BF16)
    gh_ref[...] = grad_hidden
    grads = lax.dot_general(
        grad_hidden, picked, (((0,), (0,)), ((), ())), preferred_element_type=F32
    ).astype(BF16)
    for k in range(kept):
        gv_ref[k, 0] = grads[:, k * 128 : (k + 1) * 128]


def term_kernel(rows_ref, gh_ref, w_ref, own, left, right, far_left, far_right, acc, w_all, w_sem):
    c = pl.program_id(0)
    kept = w_ref.shape[0]

    @pl.when(c == 0)
    def _():
        fetch_columns(w_ref, w_all, w_sem)
        acc[...] = jnp.zeros_like(acc)

    await_column(w_ref, w_all, w_sem, c)
    weights = jnp.concatenate([w_all[k, c] for k in range(kept)], axis=0)
    part = lax.dot_general(
        gh_ref[...], weights, (((1,), (1,)), ((), ())), preferred_element_type=F32
    )
    for k in range(kept):
        acc[rows_ref[k, c]] += part[:, k * 128 : (k + 1) * 128]

    @pl.when(c == pl.num_programs(0) - 1)
    def _():
        for ref, (start, size) in zip((own, left, right, far_left, far_right), PARTS):
            ref[...] = acc[start : start + size].astype(BF16)


def hidden_call(rows, parts, weights, grad_act):
    kept, cols = rows.shape
    n_tok = grad_act.shape[0]
    column = pl.BlockSpec((n_tok, 128), lambda c, *_: (0, c))
    all_slots = pl.BlockSpec((kept, 1, 128, 128), lambda c, *_: (0, c, 0, 0))
    wide = jax.ShapeDtypeStruct((n_tok, cols * 128), BF16)
    grads = jax.ShapeDtypeStruct((kept, cols, 128, 128), BF16)
    return pl.pallas_call(
        hidden_kernel,
        grid_spec=pltpu.PrefetchScalarGridSpec(
            num_scalar_prefetch=1,
            grid=(cols,),
            in_specs=[pl.BlockSpec(memory_space=pl.ANY)] * 5
            + [pl.BlockSpec(memory_space=pltpu.HBM), column],
            out_specs=[column, column, all_slots],
            scratch_shapes=[
                pltpu.VMEM((64, n_tok, 128), BF16),
                pltpu.VMEM((kept, cols, 128, 128), BF16),
                pltpu.SemaphoreType.DMA((5,)),
                pltpu.SemaphoreType.DMA((cols,)),
            ],
        ),
        out_shape=[wide, wide, grads],
        compiler_params=pltpu.CompilerParams(vmem_limit_bytes=18 * 2**20),
        cost_estimate=pl.CostEstimate(flops=1_073_741_824, bytes_accessed=11_000_000, transcendentals=131072),
    )(rows, *parts, weights, grad_act)


def term_call(rows, grad_hidden, weights):
    kept, cols = rows.shape
    n_tok = grad_hidden.shape[0]
    return pl.pallas_call(
        term_kernel,
        grid_spec=pltpu.PrefetchScalarGridSpec(
            num_scalar_prefetch=1,
            grid=(cols,),
            in_specs=[
                pl.BlockSpec((n_tok, 128), lambda c, rows: (0, c)),
                pl.BlockSpec(memory_space=pltpu.HBM),
            ],
            out_specs=[pl.BlockSpec((n, n_tok, 128), lambda c, rows: (0, 0, 0)) for _, n in PARTS],
            scratch_shapes=[
                pltpu.VMEM((64, n_tok, 128), F32),
                pltpu.VMEM((kept, cols, 128, 128), BF16),
                pltpu.SemaphoreType.DMA((cols,)),
            ],
        ),
        out_shape=[jax.ShapeDtypeStruct((n, n_tok, 128), BF16) for _, n in PARTS],
        compiler_params=pltpu.CompilerParams(vmem_limit_bytes=20 * 2**20),
        cost_estimate=pl.CostEstimate(flops=536_870_912, bytes_accessed=7_000_000, transcendentals=0),
    )(rows, grad_hidden, weights)


def shift(a, by):
    return lax.ppermute(a, Z, [(i, (i + by) % 16) for i in range(16)])


def total(*arrays):
    return sum(a.astype(F32) for a in arrays)


def gather_tokens(copies):
    own = lax.all_to_all(copies, FAR, 0, 0).reshape((16,) + copies.shape[2:])
    left, right = shift(own, 1), shift(own, -1)
    return own, left, right, shift(left[:8], 1), shift(right[8:], -1)


def turn_kernel(grads_ref, out_ref):
    for c in range(grads_ref.shape[0]):
        out_ref[c] = grads_ref[c].T


def order_kernel(*refs):
    pass


def held_until(x, after):
    anywhere = pl.BlockSpec(memory_space=pl.ANY)
    return pl.pallas_call(
        order_kernel,
        in_specs=[anywhere, anywhere],
        out_specs=anywhere,
        out_shape=jax.ShapeDtypeStruct(x.shape, x.dtype),
        input_output_aliases={0: 0},
        compiler_params=pltpu.CompilerParams(vmem_limit_bytes=2**20),
    )(x, after)


def near_kernel(left_ref, right_ref, from_right, from_left, left_out, right_out):
    left_out[...] = total(left_ref[...], from_right[...]).astype(BF16)
    right_out[...] = total(right_ref[...], from_left[...]).astype(BF16)


def add_near(left, right, from_right, from_left):
    n, n_tok, _ = left.shape
    first = pl.BlockSpec((n // 2, n_tok, 128), lambda i: (0, 0, 0))
    second = pl.BlockSpec((n // 2, n_tok, 128), lambda i: (1, 0, 0))
    return pl.pallas_call(
        near_kernel,
        grid=(1,),
        in_specs=[first, second, first, first],
        out_specs=[first, second],
        out_shape=[jax.ShapeDtypeStruct(left.shape, BF16)] * 2,
        input_output_aliases={0: 0, 1: 1},
        compiler_params=pltpu.CompilerParams(vmem_limit_bytes=6 * 2**20),
        cost_estimate=pl.CostEstimate(flops=500_000, bytes_accessed=1_500_000, transcendentals=0),
    )(left, right, from_right, from_left)


def own_kernel(own_ref, left_ref, right_ref, out_ref):
    out_ref[...] = total(own_ref[...], left_ref[...], right_ref[...]).astype(BF16)


def finish_kernel(far_ref, out_ref):
    summed = sum(far_ref[i].astype(F32) for i in range(far_ref.shape[0])).astype(BF16)
    out_ref[...] = jnp.concatenate([summed[0], summed[1]], axis=1)


def small_call(kernel, args, out):
    return pl.pallas_call(
        kernel,
        out_shape=out,
        compiler_params=pltpu.CompilerParams(vmem_limit_bytes=6 * 2**20),
        cost_estimate=pl.CostEstimate(flops=500_000, bytes_accessed=2_000_000, transcendentals=0),
    )(*args)


def reduce_terms(own, left, right, far_left, far_right):
    n_tok = own.shape[1]
    left, right = add_near(left, right, shift(far_left, -1), shift(far_right, 1))
    out = jax.ShapeDtypeStruct(own.shape, BF16)
    own = small_call(own_kernel, (own, shift(left, -1), shift(right, 1)), out)
    far = lax.all_to_all(own.reshape((8, 2, n_tok, 128)), FAR, 0, 0)
    return small_call(finish_kernel, (far,), jax.ShapeDtypeStruct((n_tok, 256), BF16))


def shards(tokens, block_values, block_rows, grad_act):
    n_tok = tokens.shape[0]
    cols = block_values.shape[0]
    mine = tokens.reshape(n_tok, 2, 128).transpose(1, 0, 2)
    copies = jnp.broadcast_to(mine, (8,) + mine.shape)
    parts = gather_tokens(copies)
    row_tile = jnp.zeros((16, 128), BF16).at[0, :cols].set(block_rows[:, 0].astype(BF16))
    row_tile = held_until(row_tile, copies)
    sent = jnp.concatenate([block_values.reshape(cols * 128, 128), row_tile])
    weights = lax.all_gather(sent, SEQ, axis=0)
    rows = weights[:, cols * 128, :cols].astype(jnp.int32)
    rows = (rows // 2 - lax.axis_index("zl")) % 4 * 16 + rows % 32 // 8 * 4 + rows // 32 * 2 + rows % 2
    activated, grad_hidden, grads = hidden_call(rows, parts, weights, grad_act)
    grads = lax.psum_scatter(grads, SEQ, scatter_dimension=0)
    summed = reduce_terms(*term_call(rows, grad_hidden, weights))
    grads = small_call(turn_kernel, (grads,), jax.ShapeDtypeStruct(grads.shape, BF16))
    return activated, summed, grads[:, None]


def solution(mesh):
    fine = Mesh(mesh.devices.reshape(SIZES), AXES)
    in_specs = (P(SEQ, MP), P(MP, SEQ, None, None), P(MP, SEQ), P(SEQ, MP))
    out_specs = (P(SEQ, MP), P(SEQ, MP), P(MP, SEQ, None, None))
    return jax.shard_map(shards, mesh=fine, in_specs=in_specs, out_specs=out_specs, check_vma=False)
```
